32 devices in a mesh: span: 8 (over z, y), seq: 4 (over x, core).
Axes of the slice: x: 2, y: 2, z: 4, core: 2. Of those that a mesh axis runs over, the one named last changes fastest.
Arguments:
- queries: bfloat16 [6144, 2560], P(('span', 'seq')), may hold values from -32 to 32
- keys: bfloat16 [6144, 2560], P(('span', 'seq')), may hold values from -32 to 32
- values: bfloat16 [6144, 2560], P(('span', 'seq')), may hold values from -6 to 6
- level_index: int32 [8], replicated, may hold values from 0 to 3
- plan: int32 [4], replicated, may hold values from 0 to 999
- gate_weight: float32 [256, 2560], replicated, may hold values from -0.375 to 0.375
Outputs:
- gated: bfloat16 [6144, 2560], P(('span', 'seq'))
The draws below stay inside these ranges and needn't reach their ends.
All inputs are finite; a program needn't handle non-finite values.
Results may differ from the reference program's by a relative error of at most 0.009.
Values may be sent and summed in bfloat16 or wider, within the bound.
No kernel may reach another device: no remote copies, remote signals or barrier semaphores. Data moves between devices by JAX's collectives and lax.ppermute only.
A program may use at most 192 MiB of HBM per device.

```python
import math
import jax
import jax.numpy as jnp
from jax import lax

HEADS = 20
HEAD_DIM = 128
FREQ = 256
WINDOW = 4
LEVELS = 4
SPANS = 8
SPAN_TOK = 768
TOKENS = 6144
HD = 2560


def draw_queries(key, part):
    key = jax.random.fold_in(key, 11)
    array_shape = (TOKENS, HEADS * HEAD_DIM)
    drawn = 2.5 * jax.random.normal(key, array_shape, jnp.float32)
    return jnp.clip(drawn, -32.0, 32.0).astype(jnp.bfloat16)


def draw_keys(key, part):
    key = jax.random.fold_in(key, 23)
    array_shape = (TOKENS, HEADS * HEAD_DIM)
    drawn = jax.random.normal(key, array_shape, jnp.float32)
    return jnp.clip(drawn, -32.0, 32.0).astype(jnp.bfloat16)


def set_ends(array, key, smallest, top_value):
    index_at = [jax.random.randint(jax.random.fold_in(key, axis), (), 0, length) for axis, length in enumerate(array.shape)]
    main_axis = array.shape.index(max(array.shape))
    next_to = index_at[:main_axis] + [(index_at[main_axis] + 1) % array.shape[main_axis]] + index_at[main_axis + 1:]
    return array.at[tuple(index_at)].set(smallest).at[tuple(next_to)].set(top_value)


def steps_of(stream_key, extent, shards, low, largest):
    def one(dim, parts):
        draws = jax.random.uniform(jax.random.fold_in(jax.random.fold_in(stream_key, 6), dim), (parts,), jnp.float32, low / len(shards), largest / len(shards))
        return jnp.repeat(jnp.exp(draws), extent[dim] // parts).reshape((-1,) + (1,) * (len(extent) - dim - 1))

    loudness = one(*shards[0])
    for cut in shards[1:]:
        loudness = loudness * one(*cut)
    return loudness


def bell_draw(rng, dims, spread, limit, cuts=(), kind=jnp.bfloat16):
    loudness = steps_of(rng, dims, cuts, -0.22, 0.18) if cuts else 1.0
    values = jax.random.normal(rng, dims, jnp.float32) * spread * loudness
    return jnp.minimum(jnp.maximum(values, -limit), limit).astype(kind)


def setup_inputs(seed: int = 0) -> dict:
    streams_of = jax.random.split(jax.random.key(seed), 7)
    queries = draw_queries(jax.random.fold_in(streams_of[6], 71), 0)
    keys = draw_keys(jax.random.fold_in(streams_of[6], 71), 0)
    values = bell_draw(streams_of[2], (TOKENS, HD), 1.0, 6.0, ((0, 32),))
    level_index = set_ends(jax.random.randint(streams_of[3], (SPANS,), 0, LEVELS), jax.random.fold_in(streams_of[3], 1), 0, LEVELS - 1).astype(jnp.int32)
    plan = set_ends(jax.random.randint(streams_of[4], (LEVELS,), 0, 1000), jax.random.fold_in(streams_of[4], 1), 0, 999).astype(jnp.int32)
    gate_weight = bell_draw(streams_of[5], (FREQ, HD), FREQ ** -0.5, 0.375, (), jnp.float32)
    return dict(queries=queries, keys=keys, values=values, level_index=level_index, plan=plan, gate_weight=gate_weight)


def reference(queries, keys, values, level_index, plan, gate_weight):
    half_freq = FREQ // 2
    frequencies = jnp.exp(-math.log(10000.0) * jnp.arange(half_freq, dtype=jnp.float32) / half_freq)
    timesteps = lax.optimization_barrier(jnp.sum(jnp.where(level_index[:, None] == jnp.arange(LEVELS, dtype=jnp.int32)[None, :], plan[None, :], 0), axis=1))
    angles = timesteps.astype(jnp.float32)[:, None] * frequencies[None, :]
    embedding = jnp.concatenate([jnp.cos(angles), jnp.sin(angles)], axis=1)
    gate_values = jnp.dot(embedding, gate_weight, precision=lax.Precision.HIGHEST, preferred_element_type=jnp.float32)
    score_scale = 1.0 / math.sqrt(HEAD_DIM)
    query_blocks = queries.reshape(SPANS, SPAN_TOK, HEADS, HEAD_DIM)
    padding = jnp.zeros((WINDOW, SPAN_TOK, HEADS, HEAD_DIM), keys.dtype)
    key_blocks = jnp.concatenate([padding, keys.reshape(SPANS, SPAN_TOK, HEADS, HEAD_DIM)], axis=0)
    value_blocks = jnp.concatenate([padding, values.reshape(SPANS, SPAN_TOK, HEADS, HEAD_DIM)], axis=0)

    def one_span(span_number):
        span_number = span_number.astype(jnp.int32)
        key_window = lax.dynamic_slice_in_dim(key_blocks, span_number, WINDOW + 1, 0).reshape((WINDOW + 1) * SPAN_TOK, HEADS, HEAD_DIM)
        value_window = lax.dynamic_slice_in_dim(value_blocks, span_number, WINDOW + 1, 0).reshape((WINDOW + 1) * SPAN_TOK, HEADS, HEAD_DIM)
        query_span = lax.dynamic_index_in_dim(query_blocks, span_number, 0, keepdims=False)
        usable = span_number - WINDOW + jnp.arange(WINDOW + 1, dtype=jnp.int32) >= 0
        key_mask = jnp.repeat(usable, SPAN_TOK)
        scores = jnp.einsum('qhd,khd->qhk', query_span.astype(jnp.float32), key_window.astype(jnp.float32)) * score_scale
        scores = jnp.where(key_mask[None, None, :], scores, -jnp.inf)
        row_peak = lax.optimization_barrier(jnp.max(scores, axis=2))
        weights = jnp.exp(scores - row_peak[:, :, None]).astype(jnp.bfloat16)
        denominator = lax.optimization_barrier(jnp.sum(weights.astype(jnp.float32), axis=2))
        numerator = jnp.einsum('qhk,khd->qhd', weights.astype(jnp.float32), value_window.astype(jnp.float32))
        return (numerator / denominator[:, :, None]).reshape(SPAN_TOK, HD).astype(jnp.bfloat16)
    attended = lax.map(one_span, jnp.arange(SPANS, dtype=jnp.int32))
    gated = (gate_values[:, None, :] * attended.astype(jnp.float32)).astype(jnp.bfloat16)
    return gated.reshape(TOKENS, HD)
```

```python
import functools
import math

import jax
import jax.numpy as jnp
from jax import lax
from jax.experimental import pallas as pl
from jax.experimental.pallas import tpu as pltpu
from jax.sharding import PartitionSpec as P

HEAD_DIM = 128
AXES = ("span", "seq")
ANY = pl.BlockSpec(memory_space=pl.ANY)
SMEM = pl.BlockSpec(memory_space=pltpu.SMEM)
VMEM_LIMIT = 48 * 1024 * 1024
NT = (((1,), (1,)), ((), ()))
NN = (((1,), (0,)), ((), ()))


def params():
    return pltpu.CompilerParams(vmem_limit_bytes=VMEM_LIMIT)


def move(block, target):
    spans, members = lax.axis_size("span"), lax.axis_size("seq")
    route = []
    for device in range(spans * members):
        span, member = divmod(device, members)
        to_span, to_member = target(span, member)
        if 0 <= to_span < spans:
            route.append((device, to_span * members + to_member))
    return lax.ppermute(block, AXES, route)


def within_level(dx, dy):
    return lambda span, member: (span ^ dy, member ^ (2 * dx))


def other_core(span, member):
    return span, member ^ 1


def one_up(span, member):
    return span + 2, member


def one_down(span, member):
    return span - 2, member


PLACES = ((0, 0), (0, 1), (1, 0), (1, 1))


def timestep_gate(level_index, plan, gate_weight, span_number):
    noise_level = jnp.sum(
        jnp.where(jnp.arange(level_index.shape[0], dtype=jnp.int32) == span_number, level_index, 0)
    )
    timestep = jnp.sum(
        jnp.where(jnp.arange(plan.shape[0], dtype=jnp.int32) == noise_level, plan, 0)
    )
    half_freq = gate_weight.shape[0] // 2
    frequencies = jnp.exp(-math.log(10000.0) * jnp.arange(half_freq, dtype=jnp.float32) / half_freq)
    angles = timestep.astype(jnp.float32) * frequencies
    embedding = jnp.concatenate([jnp.cos(angles), jnp.sin(angles)])[None, :]
    return jnp.dot(
        embedding, gate_weight, precision=lax.Precision.HIGHEST, preferred_element_type=jnp.float32
    )


def pack_kernel(start, width, group_width, meta, q, k, v, *rest):
    outs, sems = rest[:4], rest[4]
    copies = []
    for j in range(4):
        column = pl.multiple_of(meta[j] * group_width + start, HEAD_DIM)
        for t, ref in enumerate((q, k, v)):
            copy = pltpu.make_async_copy(
                ref.at[:, pl.ds(column, width)],
                outs[j].at[:, pl.ds(t * width, width)],
                sems.at[j, t],
            )
            copy.start()
            copies.append(copy)
    for copy in copies:
        copy.wait()


def pack(meta, q, k, v, start, width, group_width):
    rows = q.shape[0]
    return pl.pallas_call(
        functools.partial(pack_kernel, start, width, group_width),
        out_shape=[jax.ShapeDtypeStruct((rows, 3 * width), q.dtype)] * 4,
        in_specs=[SMEM, ANY, ANY, ANY],
        out_specs=[ANY] * 4,
        scratch_shapes=[pltpu.SemaphoreType.DMA((4, 3))],
        compiler_params=params(),
        cost_estimate=pl.CostEstimate(flops=0, bytes_accessed=24 * rows * width * 2, transcendentals=0),
        name="pack",
    )(meta, q, k, v)


def stack_kernel(width, meta, *refs):
    pieces, (q_out, kv_out, sems) = refs[:4], refs[4:]
    rows = pieces[0].shape[0]
    copies = []
    for j, (dx, _) in enumerate(PLACES):
        parity = meta[4 + j]
        at = pl.ds(dx * rows, rows)
        for t, (source, target) in enumerate(
            (
                (pieces[j].at[:, pl.ds(width, 2 * width)], kv_out.at[parity, at]),
                (pieces[j].at[:, pl.ds(0, width)], q_out.at[parity, at]),
            )
        ):
            copy = pltpu.make_async_copy(source, target, sems.at[j, t])
            copy.start()
            copies.append(copy)
    for copy in copies:
        copy.wait()


def stack(meta, pieces, width):
    rows = pieces[0].shape[0]
    dtype = pieces[0].dtype
    return pl.pallas_call(
        functools.partial(stack_kernel, width),
        out_shape=[
            jax.ShapeDtypeStruct((2, 2 * rows, width), dtype),
            jax.ShapeDtypeStruct((2, 2 * rows, 2 * width), dtype),
        ],
        in_specs=[SMEM] + [ANY] * 4,
        out_specs=[ANY] * 2,
        scratch_shapes=[pltpu.SemaphoreType.DMA((4, 2))],
        compiler_params=params(),
        cost_estimate=pl.CostEstimate(flops=0, bytes_accessed=24 * rows * width * 2, transcendentals=0),
        name="stack",
    )(meta, *pieces)


def softmax_part(q, keys, values):
    scale = math.log2(math.e) / math.sqrt(HEAD_DIM)
    scores = [lax.dot_general(q, k, NT, preferred_element_type=jnp.float32) for k in keys]
    peak = functools.reduce(jnp.maximum, scores).max(axis=1, keepdims=True)
    peak = peak * scale
    weights = [jnp.exp2(s * scale - peak) for s in scores]
    total = functools.reduce(jnp.add, weights).sum(axis=1, keepdims=True)
    out = functools.reduce(
        jnp.add,
        [
            lax.dot_general(w.astype(jnp.bfloat16), v, NN, preferred_element_type=jnp.float32)
            for w, v in zip(weights, values)
        ],
    )
    return out / total, peak + jnp.log2(total)


def attend_rows(q_ref, p, pairs, o_ref, lse_ref, tile):
    rows = q_ref.shape[1]
    for start in range(0, rows, tile):
        at = pl.ds(start, tile)
        out, lse = softmax_part(
            q_ref[p, at], [k[i] for k, _, i in pairs], [v[i] for _, v, i in pairs]
        )
        o_ref[p, at] = out.astype(o_ref.dtype)
        lse_ref[0, :, pl.ds(p * rows + start, tile)] = jnp.broadcast_to(lse, (tile, 128)).T[:1]


TILE = 128


def remote_kernel(q, ka, va, kb, vb, o, lse):
    every = [(ka, va, 0), (kb, vb, 0), (ka, va, 1), (kb, vb, 1)]
    attend_rows(q, 0, every, o, lse, TILE)
    attend_rows(q, 1, every[2:], o, lse, TILE)


def own_kernel(meta, q, ka, va, kb, vb, ua, xa, ub, xb, o, lse):
    own = [(ka, va, 0), (kb, vb, 0), (ka, va, 1), (kb, vb, 1)]
    above = [(ua, xa, 0), (ub, xb, 0), (ua, xa, 1), (ub, xb, 1)]

    @pl.when(meta[8] >= 1)
    def _():
        attend_rows(q, 0, own[:2] + above, o, lse, TILE)
        attend_rows(q, 1, own + above, o, lse, TILE)

    @pl.when(meta[8] < 1)
    def _():
        attend_rows(q, 0, own[:2], o, lse, TILE)
        attend_rows(q, 1, own, o, lse, TILE)


def attention(body, meta, q, kvs, units, out_dtype, name):
    _, rows, width = q.shape
    heads = width // HEAD_DIM
    block = (2, rows, HEAD_DIM)
    head = pl.BlockSpec(block, lambda h: (0, 0, h))
    value = pl.BlockSpec(block, lambda h: (0, 0, heads + h))
    operands, specs = [], []
    if meta is not None:
        operands, specs = [meta], [SMEM]
    operands.append(q)
    specs.append(head)
    for kv in kvs:
        operands += [kv, kv]
        specs += [head, value]
    scores = heads * units * rows * 2 * rows
    return pl.pallas_call(
        body,
        grid=(heads,),
        out_shape=[
            jax.ShapeDtypeStruct((2, rows, width), out_dtype),
            jax.ShapeDtypeStruct((heads, 1, 2 * rows), jnp.float32),
        ],
        in_specs=specs,
        out_specs=[head, pl.BlockSpec((1, 1, 2 * rows), lambda h: (h, 0, 0))],
        compiler_params=params(),
        cost_estimate=pl.CostEstimate(
            flops=scores * HEAD_DIM * 4, bytes_accessed=4 * rows * width * 4, transcendentals=scores
        ),
        name=name,
    )(*operands)


def merge_kernel(meta, o, lse, o_far, lse_far, *rest):
    outs, scratch = rest[:4], rest[4]
    rows = o.shape[1]
    half = rows // 2
    far = jnp.where(meta[8] >= 2, 1.0, 0.0)
    share = far / (1.0 + jnp.exp2(lse[0] - lse_far[0]))
    for p in range(2):
        weight = jnp.broadcast_to(share[:, p * rows : (p + 1) * rows], (HEAD_DIM, rows)).T
        near = o[p].astype(jnp.float32)
        scratch[p] = near + weight * (o_far[p].astype(jnp.float32) - near)
    for j, (dx, _) in enumerate(PLACES):
        outs[j][...] = scratch[meta[4 + j], pl.ds(dx * half, half)].astype(outs[j].dtype)


def merge(meta, o, lse, o_far, lse_far):
    _, rows, width = o.shape
    heads = width // HEAD_DIM
    head = pl.BlockSpec((2, rows, HEAD_DIM), lambda h: (0, 0, h))
    row = pl.BlockSpec((1, 1, 2 * rows), lambda h: (h, 0, 0))
    return pl.pallas_call(
        merge_kernel,
        grid=(heads,),
        out_shape=[jax.ShapeDtypeStruct((rows // 2, width), jnp.bfloat16)] * 4,
        in_specs=[SMEM, head, row, head, row],
        out_specs=[pl.BlockSpec((rows // 2, HEAD_DIM), lambda h: (0, h))] * 4,
        scratch_shapes=[pltpu.VMEM((2, rows, HEAD_DIM), jnp.float32)],
        compiler_params=params(),
        cost_estimate=pl.CostEstimate(
            flops=8 * rows * width, bytes_accessed=20 * rows * width, transcendentals=0
        ),
        name="merge",
    )(meta, o, lse, o_far, lse_far)


def finish_kernel(starts, group_width, meta, gate, *refs):
    pieces, out = refs[:-1], refs[-1]
    for i, piece in enumerate(pieces):
        chunk, j = divmod(i, 4)
        width = piece.shape[1]
        at = pl.ds(pl.multiple_of(meta[j] * group_width + starts[chunk], HEAD_DIM), width)
        out[:, at] = (gate[:, at] * piece[...].astype(jnp.float32)).astype(out.dtype)


def finish(meta, gate, pieces, starts, group_width):
    rows = pieces[0].shape[0]
    whole = pl.BlockSpec(memory_space=pltpu.VMEM)
    return pl.pallas_call(
        functools.partial(finish_kernel, starts, group_width),
        out_shape=jax.ShapeDtypeStruct((rows, 4 * group_width), jnp.bfloat16),
        in_specs=[SMEM] + [whole] * (1 + len(pieces)),
        out_specs=whole,
        compiler_params=params(),
        cost_estimate=pl.CostEstimate(
            flops=rows * group_width * 4, bytes_accessed=rows * group_width * 16, transcendentals=0
        ),
        name="finish",
    )(meta, gate, *pieces)


def shards(queries, keys, values, level_index, plan, gate_weight):
    span = lax.axis_index("span")
    member = lax.axis_index("seq")
    x, y = member // 2, span % 2
    group_width = queries.shape[1] // 4
    group_heads = group_width // HEAD_DIM
    meta = jnp.stack(
        [2 * (x ^ dx) + (y ^ dy) for dx, dy in PLACES]
        + [y ^ dy for _, dy in PLACES]
        + [span // 2]
    ).astype(jnp.int32)
    gate = timestep_gate(level_index, plan, gate_weight, span)

    sizes = []
    while sum(sizes) < group_heads:
        sizes.append(min(2 if sizes else 1, group_heads - sum(sizes)))
    starts = [sum(sizes[:i]) * HEAD_DIM for i in range(len(sizes))]

    results = []
    for size, start in zip(sizes, starts):
        width = size * HEAD_DIM
        sent = pack(meta, queries, keys, values, start, width, group_width)
        pieces = [sent[0]] + [move(sent[j], within_level(*PLACES[j])) for j in (1, 2, 3)]
        q, kv = stack(meta, pieces, width)
        kv_up = move(kv, one_up)
        q_down = move(q, one_down)
        kv_other = move(kv, other_core)
        kv_up_other = move(kv_up, other_core)
        o_part, lse_part = attention(
            remote_kernel, None, q_down, (kv_up, kv_up_other), 3, jnp.bfloat16, "remote"
        )
        o_far, lse_far = move(o_part, one_up), move(lse_part, one_up)
        o, lse = attention(
            own_kernel, meta, q, (kv, kv_other, kv_up, kv_up_other), 7, jnp.float32, "own"
        )
        merged = merge(meta, o, lse, o_far, lse_far)
        results += [merged[0]] + [move(merged[j], within_level(*PLACES[j])) for j in (1, 2, 3)]
    return finish(meta, gate, results, starts, group_width)


def solution(mesh):
    rows = P(AXES, None)
    return jax.shard_map(
        shards,
        mesh=mesh,
        in_specs=(rows, rows, rows, P(), P(), P()),
        out_specs=rows,
        check_vma=False,
    )
```

```python
import functools
import math

import jax
import jax.numpy as jnp
from jax import lax
from jax.experimental import pallas as pl
from jax.experimental.pallas import tpu as pltpu
from jax.sharding import PartitionSpec as P

HEAD_DIM = 128
AXES = ("span", "seq")
ANY = pl.BlockSpec(memory_space=pl.ANY)
SMEM = pl.BlockSpec(memory_space=pltpu.SMEM)
MIB = 1024 * 1024
TILE = 128
NT = (((1,), (1,)), ((), ()))
NN = (((1,), (0,)), ((), ()))


def params(mib):
    return pltpu.CompilerParams(vmem_limit_bytes=mib * MIB)


def move(block, target):
    spans, members = lax.axis_size("span"), lax.axis_size("seq")
    route = []
    for device in range(spans * members):
        span, member = divmod(device, members)
        to_span, to_member = target(span, member)
        if 0 <= to_span < spans:
            route.append((device, to_span * members + to_member))
    return lax.ppermute(block, AXES, route)


def within_level(dx, dy):
    return lambda span, member: (span ^ dy, member ^ (2 * dx))


def other_core(span, member):
    return span, member ^ 1


def one_up(span, member):
    return span + 2, member


def one_down(span, member):
    return span - 2, member


PLACES = ((0, 0), (0, 1), (1, 0), (1, 1))


def timestep_gate(level_index, plan, gate_weight, span_number):
    noise_level = jnp.sum(
        jnp.where(jnp.arange(level_index.shape[0], dtype=jnp.int32) == span_number, level_index, 0)
    )
    timestep = jnp.sum(
        jnp.where(jnp.arange(plan.shape[0], dtype=jnp.int32) == noise_level, plan, 0)
    )
    half_freq = gate_weight.shape[0] // 2
    frequencies = jnp.exp(-math.log(10000.0) * jnp.arange(half_freq, dtype=jnp.float32) / half_freq)
    angles = timestep.astype(jnp.float32) * frequencies
    embedding = jnp.concatenate([jnp.cos(angles), jnp.sin(angles)])[None, :]
    return jnp.dot(
        embedding, gate_weight, precision=lax.Precision.HIGHEST, preferred_element_type=jnp.float32
    )


def pack_kernel(first, heads, group_width, count, meta, q, k, v, *rest):
    outs, sems = rest[count : count + 4], rest[count + 4]
    copies = []
    for j in range(4):
        for t, ref in enumerate((q, k, v)):
            for h in range(heads):
                column = pl.multiple_of(meta[j] * group_width + (first + h) * HEAD_DIM, HEAD_DIM)
                copy = pltpu.make_async_copy(
                    ref.at[:, pl.ds(column, HEAD_DIM)], outs[j].at[t * heads + h], sems.at[j, t * heads + h]
                )
                copy.start()
                copies.append(copy)
    for copy in copies:
        copy.wait()


def pack(meta, q, k, v, first, heads, group_width, after):
    rows = q.shape[0]
    return pl.pallas_call(
        functools.partial(pack_kernel, first, heads, group_width, len(after)),
        out_shape=[jax.ShapeDtypeStruct((3 * heads, rows, HEAD_DIM), q.dtype)] * 4,
        in_specs=[SMEM] + [ANY] * (3 + len(after)),
        out_specs=[ANY] * 4,
        scratch_shapes=[pltpu.SemaphoreType.DMA((4, 3 * heads))],
        compiler_params=params(60),
        cost_estimate=pl.CostEstimate(
            flops=0, bytes_accessed=48 * rows * heads * HEAD_DIM, transcendentals=0
        ),
        name="pack",
    )(meta, q, k, v, *after)


def stack_kernel(heads, count, meta, *refs):
    pieces, (q_out, kv_out, sems) = refs[:4], refs[4 + count :]
    rows = pieces[0].shape[1]
    copies = []
    for j, (dx, _) in enumerate(PLACES):
        parity = meta[4 + j]
        at = pl.ds(dx * rows, rows)
        for t, (source, target) in enumerate(
            (
                (pieces[j].at[pl.ds(heads, 2 * heads)], kv_out.at[:, parity, at]),
                (pieces[j].at[pl.ds(0, heads)], q_out.at[:, parity, at]),
            )
        ):
            copy = pltpu.make_async_copy(source, target, sems.at[j, t])
            copy.start()
            copies.append(copy)
    for copy in copies:
        copy.wait()


def stack(meta, pieces, after):
    triple, rows, _ = pieces[0].shape
    heads = triple // 3
    dtype = pieces[0].dtype
    return pl.pallas_call(
        functools.partial(stack_kernel, heads, len(after)),
        out_shape=[
            jax.ShapeDtypeStruct((heads, 2, 2 * rows, HEAD_DIM), dtype),
            jax.ShapeDtypeStruct((2 * heads, 2, 2 * rows, HEAD_DIM), dtype),
        ],
        in_specs=[SMEM] + [ANY] * (4 + len(after)),
        out_specs=[ANY] * 2,
        scratch_shapes=[pltpu.SemaphoreType.DMA((4, 2))],
        compiler_params=params(8),
        cost_estimate=pl.CostEstimate(
            flops=0, bytes_accessed=48 * rows * heads * HEAD_DIM, transcendentals=0
        ),
        name="stack",
    )(meta, *pieces, *after)


def softmax_part(q, keys, values):
    scale = math.log2(math.e) / math.sqrt(HEAD_DIM)
    scores = [lax.dot_general(q, k, NT, preferred_element_type=jnp.float32) for k in keys]
    peak = functools.reduce(jnp.maximum, scores).max(axis=1, keepdims=True)
    peak = peak * scale
    weights = [jnp.exp2(s * scale - peak) for s in scores]
    total = functools.reduce(jnp.add, weights).sum(axis=1, keepdims=True)
    out = functools.reduce(
        jnp.add,
        [
            lax.dot_general(w.astype(jnp.bfloat16), v, NN, preferred_element_type=jnp.float32)
            for w, v in zip(weights, values)
        ],
    )
    return out / total, peak + jnp.log2(total)


def attend_rows(q_ref, p, blocks, o_ref, lse_ref):
    rows = q_ref.shape[2]
    for t in range(rows // TILE):
        out, lse = softmax_part(
            q_ref[0, p, pl.ds(t * TILE, TILE)],
            [kv[0][0, i] for kv, i in blocks],
            [kv[1][0, i] for kv, i in blocks],
        )
        row = p * (rows // TILE) + t
        o_ref[0, pl.ds(row * TILE, TILE)] = out.astype(o_ref.dtype)
        lse_ref[pl.ds(row, 1)] = jnp.broadcast_to(lse, (TILE, TILE)).T[:1]


def remote_kernel(count, q, ka, va, kb, vb, *rest):
    o, lse = rest[count:]
    a, b = (ka, va), (kb, vb)
    every = [(a, 0), (b, 0), (a, 1), (b, 1)]
    attend_rows(q, 0, every, o, lse)
    attend_rows(q, 1, every[2:], o, lse)
    left, terms = lse[...], []
    for _ in range(3):
        terms.append(left.astype(jnp.bfloat16))
        left = left - terms[-1].astype(jnp.float32)
    terms.append(jnp.zeros_like(terms[0]))
    last = 2 * q.shape[2]
    o[0, pl.ds(last, 4 * lse.shape[0])] = jnp.concatenate(
        [term.astype(jnp.float32) for term in terms], axis=0
    ).astype(jnp.bfloat16)


def own_kernel(count, meta, q, ka, va, kb, vb, ua, xa, ub, xb, *rest):
    o, lse = rest[count:]
    a, b, c, d = (ka, va), (kb, vb), (ua, xa), (ub, xb)
    own = [(a, 0), (b, 0), (a, 1), (b, 1)]
    below = [(c, 0), (d, 0), (c, 1), (d, 1)]

    @pl.when(meta[8] >= 1)
    def _():
        attend_rows(q, 0, own[:2] + below, o, lse.at[0])
        attend_rows(q, 1, own + below, o, lse.at[0])

    @pl.when(meta[8] < 1)
    def _():
        attend_rows(q, 0, own[:2], o, lse.at[0])
        attend_rows(q, 1, own, o, lse.at[0])


def lse_rows(rows):
    return -(-2 * rows // TILE // 8) * 8


def attend(far, meta, q, kvs, after):
    heads, _, rows, _ = q.shape
    block = (1, 2, rows, HEAD_DIM)
    head = pl.BlockSpec(block, lambda h: (h, 0, 0, 0))
    value = pl.BlockSpec(block, lambda h: (heads + h, 0, 0, 0))
    operands, specs = ([], []) if far else ([meta], [SMEM])
    operands.append(q)
    specs.append(head)
    for kv in kvs:
        operands += [kv, kv]
        specs += [head, value]
    extra = lse_rows(rows)
    if far:
        length = 2 * rows + 4 * extra
        out_shape = jax.ShapeDtypeStruct((heads, length, HEAD_DIM), jnp.bfloat16)
        out_specs = pl.BlockSpec((1, length, HEAD_DIM), lambda h: (h, 0, 0))
        scratch = [pltpu.VMEM((extra, TILE), jnp.float32)]
    else:
        out_shape = [
            jax.ShapeDtypeStruct((heads, 2 * rows, HEAD_DIM), jnp.float32),
            jax.ShapeDtypeStruct((heads, extra, TILE), jnp.float32),
        ]
        out_specs = [
            pl.BlockSpec((1, 2 * rows, HEAD_DIM), lambda h: (h, 0, 0)),
            pl.BlockSpec((1, extra, TILE), lambda h: (h, 0, 0)),
        ]
        scratch = []
    scores = heads * (3 if far else 7) * rows * 2 * rows
    return pl.pallas_call(
        functools.partial(remote_kernel if far else own_kernel, len(after)),
        grid=(heads,),
        out_shape=out_shape,
        in_specs=specs + [ANY] * len(after),
        out_specs=out_specs,
        scratch_shapes=scratch,
        compiler_params=params(20),
        cost_estimate=pl.CostEstimate(
            flops=scores * HEAD_DIM * 4,
            bytes_accessed=(len(kvs) + 1) * heads * rows * 8 * HEAD_DIM,
            transcendentals=scores,
        ),
        name="remote" if far else "own",
    )(*operands, *after)


def merge_kernel(count, meta, o, lse, o_far, *rest):
    outs, scratch = rest[count : count + 4], rest[count + 4]
    rows = o.shape[1] // 2
    half = rows // 2
    extra = lse.shape[1]
    terms = o_far[0, pl.ds(2 * rows, 4 * extra)].astype(jnp.float32)
    lse_far = terms[:extra] + terms[extra : 2 * extra] + terms[2 * extra : 3 * extra]
    far = jnp.where(meta[8] >= 2, 1.0, 0.0)
    share = far / (1.0 + jnp.exp2(lse[0] - lse_far))
    for row in range(2 * rows // TILE):
        at = pl.ds(row * TILE, TILE)
        weight = jnp.broadcast_to(share[row : row + 1], (HEAD_DIM, TILE)).T
        near = o[0, at]
        scratch[at] = near + weight * (o_far[0, at].astype(jnp.float32) - near)
    for j, (dx, _) in enumerate(PLACES):
        at = pl.ds(pl.multiple_of(meta[4 + j] * rows + dx * half, half), half)
        outs[j][0] = scratch[at].astype(outs[j].dtype)


def merge(meta, o, lse, o_far, after):
    heads, both, _ = o.shape
    by_head = lambda h: (h, 0, 0)
    return pl.pallas_call(
        functools.partial(merge_kernel, len(after)),
        grid=(heads,),
        out_shape=[jax.ShapeDtypeStruct((heads, both // 4, HEAD_DIM), jnp.bfloat16)] * 4,
        in_specs=[SMEM]
        + [pl.BlockSpec((1,) + a.shape[1:], by_head) for a in (o, lse, o_far)]
        + [ANY] * len(after),
        out_specs=[pl.BlockSpec((1, both // 4, HEAD_DIM), by_head)] * 4,
        scratch_shapes=[pltpu.VMEM((both, HEAD_DIM), jnp.float32)],
        compiler_params=params(12),
        cost_estimate=pl.CostEstimate(
            flops=4 * both * HEAD_DIM * heads,
            bytes_accessed=8 * both * HEAD_DIM * heads,
            transcendentals=0,
        ),
        name="merge",
    )(meta, o, lse, o_far, *after)


def finish_kernel(firsts, group_width, meta, gate, *refs):
    pieces, out = refs[:-1], refs[-1]
    for i, piece in enumerate(pieces):
        chunk, j = divmod(i, 4)
        for h in range(piece.shape[0]):
            column = meta[j] * group_width + (firsts[chunk] + h) * HEAD_DIM
            at = pl.ds(pl.multiple_of(column, HEAD_DIM), HEAD_DIM)
            out[:, at] = (gate[:, at] * piece[h].astype(jnp.float32)).astype(out.dtype)


def finish(meta, gate, pieces, firsts, group_width):
    rows = pieces[0].shape[1]
    whole = pl.BlockSpec(memory_space=pltpu.VMEM)
    return pl.pallas_call(
        functools.partial(finish_kernel, firsts, group_width),
        out_shape=jax.ShapeDtypeStruct((rows, 4 * group_width), jnp.bfloat16),
        in_specs=[SMEM] + [whole] * (1 + len(pieces)),
        out_specs=whole,
        compiler_params=params(16),
        cost_estimate=pl.CostEstimate(
            flops=rows * group_width * 4, bytes_accessed=rows * group_width * 16, transcendentals=0
        ),
        name="finish",
    )(meta, gate, *pieces)


def shards(queries, keys, values, level_index, plan, gate_weight):
    span = lax.axis_index("span")
    member = lax.axis_index("seq")
    x, y = member // 2, span % 2
    group_width = queries.shape[1] // 4
    group_heads = group_width // HEAD_DIM
    meta = jnp.stack(
        [2 * (x ^ dx) + (y ^ dy) for dx, dy in PLACES]
        + [y ^ dy for _, dy in PLACES]
        + [span // 2]
    ).astype(jnp.int32)
    gate = timestep_gate(level_index, plan, gate_weight, span)

    sizes = []
    while sum(sizes) < group_heads:
        sizes.append(min(2 if sizes else 1, group_heads - sum(sizes)))
    firsts = [sum(sizes[:i]) for i in range(len(sizes))]
    chunks = range(len(sizes))

    received, last = [], []
    for i in chunks:
        sent = pack(meta, queries, keys, values, firsts[i], sizes[i], group_width, last)
        last = [sent[0]]
        received.append([sent[0]] + [move(sent[j], within_level(*PLACES[j])) for j in (1, 2, 3)])
    last.append(gate)

    q, kv, kv_up, q_down = {}, {}, {}, {}

    def spread(i, after):
        q[i], kv[i] = stack(meta, received[i], after)
        kv_up[i] = move(kv[i], one_up)
        q_down[i] = move(q[i], one_down)
        kv[i] = (kv[i], move(kv[i], other_core))
        return [q[i]]

    far, near, results = {}, {}, {}

    def remote(i, after):
        kv_up[i] = (kv_up[i], move(kv_up[i], other_core))
        far[i] = attend(True, meta, q_down[i], kv_up[i], after)
        kept = [far[i]]
        far[i] = move(far[i], one_up)
        return kept

    def own(i, after):
        near[i] = attend(False, meta, q[i], kv[i] + kv_up[i], after)
        return [near[i][1]]

    def close(i, after):
        merged = merge(meta, *near[i], far[i], after)
        results[i] = [merged[0]] + [move(merged[j], within_level(*PLACES[j])) for j in (1, 2, 3)]
        return [merged[0]]

    steps = []
    for i in chunks:
        steps.append((2 * i, spread, i))
        steps.append((2 * i + 3, remote, i))
        steps.append((2 * i + 4.5, own, i))
        steps.append((2 * i + 6.7, close, i))
    for _, step, i in sorted(steps, key=lambda item: item[0]):
        last = step(i, last)
    return finish(meta, gate, sum((results[i] for i in chunks), []), firsts, group_width)


def solution(mesh):
    rows = P(AXES, None)
    return jax.shard_map(
        shards,
        mesh=mesh,
        in_specs=(rows, rows, rows, P(), P(), P()),
        out_specs=rows,
        check_vma=False,
    )
```

```python
import functools
import math

import jax
import jax.numpy as jnp
from jax import lax
from jax.experimental import pallas as pl
from jax.experimental.pallas import tpu as pltpu
from jax.sharding import PartitionSpec as P

HEAD_DIM = 128
AXES = ("span", "seq")
ANY = pl.BlockSpec(memory_space=pl.ANY)
SMEM = pl.BlockSpec(memory_space=pltpu.SMEM)
MIB = 1024 * 1024
TILE = 128
SIZES = (3, 2)
COST = 1000
ORDER = "s0 n0 s10 n1 r0 f01 r1 f1 c0 c1"
NT = (((1,), (1,)), ((), ()))
NN = (((1,), (0,)), ((), ()))


def params(mib):
    return pltpu.CompilerParams(vmem_limit_bytes=mib * MIB)


def move(block, target):
    spans, members = lax.axis_size("span"), lax.axis_size("seq")
    route = []
    for device in range(spans * members):
        span, member = divmod(device, members)
        to_span, to_member = target(span, member)
        if 0 <= to_span < spans:
            route.append((device, to_span * members + to_member))
    return lax.ppermute(block, AXES, route)


def within_level(dx, dy):
    return lambda span, member: (span ^ dy, member ^ (2 * dx))


def other_core(span, member):
    return span, member ^ 1


def one_up(span, member):
    return span + 2, member


def one_down(span, member):
    return span - 2, member


PLACES = ((0, 0), (0, 1), (1, 0), (1, 1))


def timestep_gate(level_index, plan, gate_weight, span_number):
    noise_level = jnp.sum(
        jnp.where(jnp.arange(level_index.shape[0], dtype=jnp.int32) == span_number, level_index, 0)
    )
    timestep = jnp.sum(
        jnp.where(jnp.arange(plan.shape[0], dtype=jnp.int32) == noise_level, plan, 0)
    )
    half_freq = gate_weight.shape[0] // 2
    frequencies = jnp.exp(-math.log(10000.0) * jnp.arange(half_freq, dtype=jnp.float32) / half_freq)
    angles = timestep.astype(jnp.float32) * frequencies
    embedding = jnp.concatenate([jnp.cos(angles), jnp.sin(angles)])[None, :]
    return jnp.dot(
        embedding, gate_weight, precision=lax.Precision.HIGHEST, preferred_element_type=jnp.float32
    )


def pack_kernel(firsts, sizes, group_width, meta, q, k, v, *outs):
    for i, (first, heads) in enumerate(zip(firsts, sizes)):
        for j in range(4):
            for t, ref in enumerate((q, k, v)):
                for h in range(heads):
                    column = meta[j] * group_width + (first + h) * HEAD_DIM
                    at = pl.ds(pl.multiple_of(column, HEAD_DIM), HEAD_DIM)
                    outs[4 * i + j][t * heads + h] = ref[:, at]


def pack(meta, q, k, v, firsts, sizes, group_width):
    rows = q.shape[0]
    whole = pl.BlockSpec(memory_space=pltpu.VMEM)
    outs = pl.pallas_call(
        functools.partial(pack_kernel, firsts, sizes, group_width),
        out_shape=[
            jax.ShapeDtypeStruct((3 * heads, rows, HEAD_DIM), q.dtype)
            for heads in sizes
            for _ in PLACES
        ],
        in_specs=[SMEM, whole, whole, whole],
        out_specs=[whole] * (4 * len(sizes)),
        compiler_params=params(60),
        cost_estimate=pl.CostEstimate(flops=COST, bytes_accessed=COST, transcendentals=0),
        name="pack",
    )(meta, q, k, v)
    return [outs[4 * i : 4 * i + 4] for i in range(len(sizes))]


def stack_kernel(heads, count, meta, *refs):
    pieces, outs = refs[:4], refs[4 + count :]
    (q_out, kv_out), sems = outs[:2], outs[-1]
    rows = pieces[0].shape[1]
    copies = []
    for j, (dx, _) in enumerate(PLACES):
        parity = meta[4 + j]
        at = pl.ds(dx * rows, rows)
        for t, (source, target) in enumerate(
            (
                (pieces[j].at[pl.ds(heads, 2 * heads)], kv_out.at[:, parity, at]),
                (pieces[j].at[pl.ds(0, heads)], q_out.at[:, parity, at]),
            )
        ):
            copy = pltpu.make_async_copy(source, target, sems.at[j, t])
            copy.start()
            copies.append(copy)
    for copy in copies:
        copy.wait()


def stack(meta, pieces, later, after):
    triple, rows, _ = pieces[0].shape
    heads = triple // 3
    dtype = pieces[0].dtype
    outs = pl.pallas_call(
        functools.partial(stack_kernel, heads, len(later) + len(after)),
        out_shape=[
            jax.ShapeDtypeStruct((heads, 2, 2 * rows, HEAD_DIM), dtype),
            jax.ShapeDtypeStruct((2 * heads, 2, 2 * rows, HEAD_DIM), dtype),
        ]
        + [jax.ShapeDtypeStruct(block.shape, block.dtype) for block in later],
        in_specs=[SMEM] + [ANY] * (4 + len(later) + len(after)),
        out_specs=[ANY] * (2 + len(later)),
        scratch_shapes=[pltpu.SemaphoreType.DMA((4, 2))],
        input_output_aliases={5 + n: 2 + n for n in range(len(later))},
        compiler_params=params(8),
        cost_estimate=pl.CostEstimate(flops=COST, bytes_accessed=COST, transcendentals=0),
        name="stack",
    )(meta, *pieces, *later, *after)
    return outs[0], outs[1], outs[2:]


def softmax_part(q, keys, values):
    scale = math.log2(math.e) / math.sqrt(HEAD_DIM)
    scores = [lax.dot_general(q, k, NT, preferred_element_type=jnp.float32) for k in keys]
    peak = functools.reduce(jnp.maximum, scores).max(axis=1, keepdims=True)
    peak = peak * scale
    weights = [jnp.exp2(s * scale - peak) for s in scores]
    total = functools.reduce(jnp.add, weights).sum(axis=1, keepdims=True)
    out = functools.reduce(
        jnp.add,
        [
            lax.dot_general(w.astype(jnp.bfloat16), v, NN, preferred_element_type=jnp.float32)
            for w, v in zip(weights, values)
        ],
    )
    return out / total, peak + jnp.log2(total)


def attend_rows(q_ref, p, blocks, o_ref, lse_ref):
    rows = q_ref.shape[2]
    out, lse = softmax_part(
        q_ref[0, p], [kv[0][0, i] for kv, i in blocks], [kv[1][0, i] for kv, i in blocks]
    )
    o_ref[0, pl.ds(p * rows, rows)] = out.astype(o_ref.dtype)
    for t in range(rows // TILE):
        column = jnp.broadcast_to(lse[t * TILE : (t + 1) * TILE], (TILE, TILE))
        lse_ref[pl.ds(p * (rows // TILE) + t, 1)] = column.T[:1]


def remote_kernel(count, q, ka, va, kb, vb, *rest):
    o, lse = rest[count:]
    a, b = (ka, va), (kb, vb)
    every = [(a, 0), (b, 0), (a, 1), (b, 1)]
    attend_rows(q, 0, every, o, lse)
    attend_rows(q, 1, every[2:], o, lse)
    left, terms = lse[...], []
    for _ in range(3):
        terms.append(left.astype(jnp.bfloat16))
        left = left - terms[-1].astype(jnp.float32)
    terms.append(jnp.zeros_like(terms[0]))
    last = 2 * q.shape[2]
    o[0, pl.ds(last, 4 * lse.shape[0])] = jnp.concatenate(
        [term.astype(jnp.float32) for term in terms], axis=0
    ).astype(jnp.bfloat16)


def near_kernel(count, q, ka, va, kb, vb, *rest):
    o, lse = rest[count:]
    a, b = (ka, va), (kb, vb)
    own = [(a, 0), (b, 0), (a, 1), (b, 1)]
    attend_rows(q, 0, own[:2], o, lse.at[0])
    attend_rows(q, 1, own, o, lse.at[0])


def blend(first, first_lse, other, other_lse, usable, store):
    share = jnp.where(usable, 1.0, 0.0) / (1.0 + jnp.exp2(first_lse - other_lse))
    for row in range(first.shape[1] // TILE):
        at = pl.ds(row * TILE, TILE)
        weight = jnp.broadcast_to(share[row : row + 1], (HEAD_DIM, TILE)).T
        start = first[0, at]
        store(at, start + weight * (other[0, at].astype(jnp.float32) - start))
    more = jnp.log2(1.0 + jnp.exp2(-jnp.abs(first_lse - other_lse)))
    return jnp.where(usable, jnp.maximum(first_lse, other_lse) + more, first_lse)


def far_kernel(count, meta, q, ka, va, kb, vb, o_near, lse_near, *rest):
    o, lse, part, part_lse = rest[count:]
    a, b = (ka, va), (kb, vb)
    every = [(a, 0), (b, 0), (a, 1), (b, 1)]

    def store(at, block):
        o[0, at] = block

    @pl.when(meta[8] >= 1)
    def _():
        attend_rows(q, 0, every, part, part_lse)
        attend_rows(q, 1, every, part, part_lse)
        lse[0] = blend(o_near, lse_near[0], part, part_lse[...], True, store)

    @pl.when(meta[8] < 1)
    def _():
        o[...] = o_near[...]
        lse[...] = lse_near[...]


def in_order_kernel(*refs):
    pass


def in_order(block, after):
    return pl.pallas_call(
        in_order_kernel,
        out_shape=jax.ShapeDtypeStruct(block.shape, block.dtype),
        in_specs=[ANY] * (1 + len(after)),
        out_specs=ANY,
        input_output_aliases={0: 0},
        compiler_params=params(1),
        cost_estimate=pl.CostEstimate(flops=COST, bytes_accessed=COST, transcendentals=0),
        name="in_order",
    )(block, *after)


def lse_rows(rows):
    return -(-2 * rows // TILE // 8) * 8


def attend(body, meta, q, kv, near, after):
    heads, _, rows, _ = q.shape
    block = (1, 2, rows, HEAD_DIM)
    head = pl.BlockSpec(block, lambda h: (h, 0, 0, 0))
    value = pl.BlockSpec(block, lambda h: (heads + h, 0, 0, 0))
    extra = lse_rows(rows)
    by_head = lambda h: (h, 0, 0)
    o_spec = pl.BlockSpec((1, 2 * rows, HEAD_DIM), by_head)
    lse_spec = pl.BlockSpec((1, extra, TILE), by_head)
    part_lse = pltpu.VMEM((extra, TILE), jnp.float32)
    operands = [q] + [half for half in kv for _ in range(2)]
    specs = [head] + [head, value] * 2
    out_shape = [
        jax.ShapeDtypeStruct((heads, 2 * rows, HEAD_DIM), jnp.float32),
        jax.ShapeDtypeStruct((heads, extra, TILE), jnp.float32),
    ]
    out_specs, scratch = [o_spec, lse_spec], []
    if body is remote_kernel:
        length = 2 * rows + 4 * extra
        out_shape = jax.ShapeDtypeStruct((heads, length, HEAD_DIM), jnp.bfloat16)
        out_specs = pl.BlockSpec((1, length, HEAD_DIM), by_head)
        scratch = [part_lse]
    if body is far_kernel:
        operands = [meta] + operands + list(near)
        specs = [SMEM] + specs + [o_spec, lse_spec]
        scratch = [pltpu.VMEM((1, 2 * rows, HEAD_DIM), jnp.float32), part_lse]
    return pl.pallas_call(
        functools.partial(body, len(after)),
        grid=(heads,),
        out_shape=out_shape,
        in_specs=specs + [ANY] * len(after),
        out_specs=out_specs,
        scratch_shapes=scratch,
        compiler_params=params(20),
        cost_estimate=pl.CostEstimate(flops=COST, bytes_accessed=COST, transcendentals=0),
        name=body.__name__[:-7],
    )(*operands, *after)


def merge_kernel(count, meta, o, lse, o_far, *rest):
    outs, scratch = rest[count : count + 4], rest[count + 4]
    rows = o.shape[1] // 2
    half = rows // 2
    extra = lse.shape[1]
    terms = o_far[0, pl.ds(2 * rows, 4 * extra)].astype(jnp.float32)
    lse_far = terms[:extra] + terms[extra : 2 * extra] + terms[2 * extra : 3 * extra]

    def store(at, block):
        scratch[at] = block

    blend(o, lse[0], o_far, lse_far, meta[8] >= 2, store)
    for j, (dx, _) in enumerate(PLACES):
        at = pl.ds(pl.multiple_of(meta[4 + j] * rows + dx * half, half), half)
        outs[j][0] = scratch[at].astype(outs[j].dtype)


def merge(meta, o, lse, o_far, after):
    heads, both, _ = o.shape
    by_head = lambda h: (h, 0, 0)
    return pl.pallas_call(
        functools.partial(merge_kernel, len(after)),
        grid=(heads,),
        out_shape=[jax.ShapeDtypeStruct((heads, both // 4, HEAD_DIM), jnp.bfloat16)] * 4,
        in_specs=[SMEM]
        + [pl.BlockSpec((1,) + a.shape[1:], by_head) for a in (o, lse, o_far)]
        + [ANY] * len(after),
        out_specs=[pl.BlockSpec((1, both // 4, HEAD_DIM), by_head)] * 4,
        scratch_shapes=[pltpu.VMEM((both, HEAD_DIM), jnp.float32)],
        compiler_params=params(12),
        cost_estimate=pl.CostEstimate(flops=COST, bytes_accessed=COST, transcendentals=0),
        name="merge",
    )(meta, o, lse, o_far, *after)


def finish_kernel(firsts, group_width, meta, gate, *refs):
    pieces, out = refs[:-1], refs[-1]
    for i, piece in enumerate(pieces):
        chunk, j = divmod(i, 4)
        for h in range(piece.shape[0]):
            column = meta[j] * group_width + (firsts[chunk] + h) * HEAD_DIM
            at = pl.ds(pl.multiple_of(column, HEAD_DIM), HEAD_DIM)
            out[:, at] = (gate[:, at] * piece[h].astype(jnp.float32)).astype(out.dtype)


def finish(meta, gate, pieces, firsts, group_width):
    rows = pieces[0].shape[1]
    whole = pl.BlockSpec(memory_space=pltpu.VMEM)
    return pl.pallas_call(
        functools.partial(finish_kernel, firsts, group_width),
        out_shape=jax.ShapeDtypeStruct((rows, 4 * group_width), jnp.bfloat16),
        in_specs=[SMEM] + [whole] * (1 + len(pieces)),
        out_specs=whole,
        compiler_params=params(16),
        cost_estimate=pl.CostEstimate(flops=COST, bytes_accessed=COST, transcendentals=0),
        name="finish",
    )(meta, gate, *pieces)


def chunk_sizes(heads):
    sizes = []
    for size in SIZES:
        if sum(sizes) + size <= heads:
            sizes.append(size)
    return sizes + [1] * (heads - sum(sizes))


def shards(queries, keys, values, level_index, plan, gate_weight):
    span = lax.axis_index("span")
    member = lax.axis_index("seq")
    x, y = member // 2, span % 2
    group_width = queries.shape[1] // 4
    group_heads = group_width // HEAD_DIM
    meta = jnp.stack(
        [2 * (x ^ dx) + (y ^ dy) for dx, dy in PLACES]
        + [y ^ dy for _, dy in PLACES]
        + [span // 2]
    ).astype(jnp.int32)
    gate = timestep_gate(level_index, plan, gate_weight, span)

    sizes = chunk_sizes(group_heads)
    firsts = [sum(sizes[:i]) for i in range(len(sizes))]
    chunks = range(len(sizes))

    sent = pack(meta, queries, keys, values, firsts, sizes, group_width)
    last = [gate]

    q, kv, kv_up, q_down = {}, {}, {}, {}
    far, own, results = {}, {}, {}

    def exchange(blocks):
        return [blocks[0]] + [move(blocks[j], within_level(*PLACES[j])) for j in (1, 2, 3)]

    exchanged = {0: exchange(sent[0])}

    def spread(i, after):
        pieces = exchanged.pop(i)
        later = sent[i + 1] if i + 1 < len(sizes) else []
        q[i], kv[i], later = stack(meta, pieces, later[1:], after)
        if later:
            exchanged[i + 1] = exchange([sent[i + 1][0], *later])
        kv_up[i] = move(kv[i], one_up)
        q_down[i] = move(q[i], one_down)
        kv[i] = (kv[i], move(kv[i], other_core))
        return [q[i]]

    def near(i, after):
        own[i] = attend(near_kernel, meta, q[i], kv[i], None, after)
        return [own[i][1]]

    def remote(i, after):
        held = in_order(kv_up[i], after)
        kv_up[i] = (held, move(held, other_core))
        part = attend(remote_kernel, meta, q_down[i], kv_up[i], None, [])
        far[i] = move(part, one_up)
        return [part]

    def own_far(i, after):
        own[i] = attend(far_kernel, meta, q[i], kv_up[i], own[i], after)
        return [own[i][1]]

    def close(i, after):
        merged = merge(meta, *own[i], far[i], after)
        results[i] = exchange(merged)
        return [merged[0]]

    steps = {"s": spread, "n": near, "r": remote, "f": own_far, "c": close}
    for step in ORDER.split():
        kind, i = step[0], int(step[1])
        extra = [q_down[int(j)] for j in step[2:]]
        last = steps[kind](i, last + extra)
    return finish(meta, gate, sum((results[i] for i in chunks), []), firsts, group_width)


def solution(mesh):
    rows = P(AXES, None)
    return jax.shard_map(
        shards,
        mesh=mesh,
        in_specs=(rows, rows, rows, P(), P(), P()),
        out_specs=rows,
        check_vma=False,
    )
```

```python
import functools
import math

import jax
import jax.numpy as jnp
from jax import lax
from jax.experimental import pallas as pl
from jax.experimental.pallas import tpu as pltpu
from jax.sharding import PartitionSpec as P

HEAD_DIM = 128
AXES = ("span", "seq")
ANY = pl.BlockSpec(memory_space=pl.ANY)
SMEM = pl.BlockSpec(memory_space=pltpu.SMEM)
MIB = 1024 * 1024
TILE = 128
SIZES = (3, 2)
APART = (0,)
COSTS = {}
EARLY = False
ORDER = "s0 n0 s1+q0 r0 n1+q1 r1 f0 f1 c0 c1"
NT = (((1,), (1,)), ((), ()))
NN = (((1,), (0,)), ((), ()))


def params(mib):
    return pltpu.CompilerParams(vmem_limit_bytes=mib * MIB)


def estimate(microseconds):
    return pl.CostEstimate(
        flops=0, bytes_accessed=int(microseconds * 3.6e6) + 1000, transcendentals=0
    )


def move(block, target):
    spans, members = lax.axis_size("span"), lax.axis_size("seq")
    route = []
    for device in range(spans * members):
        span, member = divmod(device, members)
        to_span, to_member = target(span, member)
        if 0 <= to_span < spans:
            route.append((device, to_span * members + to_member))
    return lax.ppermute(block, AXES, route)


def within_level(dx, dy):
    return lambda span, member: (span ^ dy, member ^ (2 * dx))


def other_core(span, member):
    return span, member ^ 1


def one_up(span, member):
    return span + 2, member


def one_down(span, member):
    return span - 2, member


PLACES = ((0, 0), (0, 1), (1, 0), (1, 1))


def timestep_gate(level_index, plan, gate_weight, span_number):
    noise_level = jnp.sum(
        jnp.where(jnp.arange(level_index.shape[0], dtype=jnp.int32) == span_number, level_index, 0)
    )
    timestep = jnp.sum(
        jnp.where(jnp.arange(plan.shape[0], dtype=jnp.int32) == noise_level, plan, 0)
    )
    half_freq = gate_weight.shape[0] // 2
    frequencies = jnp.exp(-math.log(10000.0) * jnp.arange(half_freq, dtype=jnp.float32) / half_freq)
    angles = timestep.astype(jnp.float32) * frequencies
    embedding = jnp.concatenate([jnp.cos(angles), jnp.sin(angles)])[None, :]
    return jnp.dot(
        embedding, gate_weight, precision=lax.Precision.HIGHEST, preferred_element_type=jnp.float32
    )


def pack_kernel(firsts, sizes, group_width, meta, q, k, v, *outs):
    for i, (first, heads) in enumerate(zip(firsts, sizes)):
        for j in range(4):
            for t, ref in enumerate((q, k, v)):
                for h in range(heads):
                    column = meta[j] * group_width + (first + h) * HEAD_DIM
                    at = pl.ds(pl.multiple_of(column, HEAD_DIM), HEAD_DIM)
                    outs[4 * i + j][t * heads + h] = ref[:, at]


def pack(meta, q, k, v, firsts, sizes, group_width, cost=0):
    rows = q.shape[0]
    whole = pl.BlockSpec(memory_space=pltpu.VMEM)
    outs = pl.pallas_call(
        functools.partial(pack_kernel, firsts, sizes, group_width),
        out_shape=[
            jax.ShapeDtypeStruct((3 * heads, rows, HEAD_DIM), q.dtype)
            for heads in sizes
            for _ in PLACES
        ],
        in_specs=[SMEM, whole, whole, whole],
        out_specs=[whole] * (4 * len(sizes)),
        compiler_params=params(60),
        cost_estimate=estimate(cost),
        name="pack",
    )(meta, q, k, v)
    return [outs[4 * i : 4 * i + 4] for i in range(len(sizes))]


def stack_kernel(heads, count, meta, *refs):
    pieces, outs = refs[:4], refs[4 + count :]
    (q_out, kv_out), sems = outs[:2], outs[-1]
    rows = pieces[0].shape[1]
    copies = []
    for j, (dx, _) in enumerate(PLACES):
        parity = meta[4 + j]
        at = pl.ds(dx * rows, rows)
        for t, (source, target) in enumerate(
            (
                (pieces[j].at[pl.ds(heads, 2 * heads)], kv_out.at[:, parity, at]),
                (pieces[j].at[pl.ds(0, heads)], q_out.at[:, parity, at]),
            )
        ):
            copy = pltpu.make_async_copy(source, target, sems.at[j, t])
            copy.start()
            copies.append(copy)
    for copy in copies:
        copy.wait()


def stack(meta, pieces, later, after, cost):
    triple, rows, _ = pieces[0].shape
    heads = triple // 3
    dtype = pieces[0].dtype
    outs = pl.pallas_call(
        functools.partial(stack_kernel, heads, len(later) + len(after)),
        out_shape=[
            jax.ShapeDtypeStruct((heads, 2, 2 * rows, HEAD_DIM), dtype),
            jax.ShapeDtypeStruct((2 * heads, 2, 2 * rows, HEAD_DIM), dtype),
        ]
        + [jax.ShapeDtypeStruct(block.shape, block.dtype) for block in later],
        in_specs=[SMEM] + [ANY] * (4 + len(later) + len(after)),
        out_specs=[ANY] * (2 + len(later)),
        scratch_shapes=[pltpu.SemaphoreType.DMA((4, 2))],
        input_output_aliases={5 + n: 2 + n for n in range(len(later))},
        compiler_params=params(8),
        cost_estimate=estimate(cost),
        name="stack",
    )(meta, *pieces, *later, *after)
    return outs[0], outs[1], outs[2:]


def softmax_part(q, keys, values):
    scale = math.log2(math.e) / math.sqrt(HEAD_DIM)
    scores = [lax.dot_general(q, k, NT, preferred_element_type=jnp.float32) for k in keys]
    peak = functools.reduce(jnp.maximum, scores).max(axis=1, keepdims=True)
    peak = peak * scale
    weights = [jnp.exp2(s * scale - peak) for s in scores]
    total = functools.reduce(jnp.add, weights).sum(axis=1, keepdims=True)
    out = functools.reduce(
        jnp.add,
        [
            lax.dot_general(w.astype(jnp.bfloat16), v, NN, preferred_element_type=jnp.float32)
            for w, v in zip(weights, values)
        ],
    )
    return out / total, peak + jnp.log2(total)


def attend_rows(q_ref, p, blocks, o_ref, lse_ref):
    rows = q_ref.shape[2]
    out, lse = softmax_part(
        q_ref[0, p], [kv[0][0, i] for kv, i in blocks], [kv[1][0, i] for kv, i in blocks]
    )
    o_ref[0, pl.ds(p * rows, rows)] = out.astype(o_ref.dtype)
    for t in range(rows // TILE):
        column = jnp.broadcast_to(lse[t * TILE : (t + 1) * TILE], (TILE, TILE))
        lse_ref[pl.ds(p * (rows // TILE) + t, 1)] = column.T[:1]


def remote_kernel(count, q, ka, va, kb, vb, *rest):
    o, lse = rest[count:]
    a, b = (ka, va), (kb, vb)
    every = [(a, 0), (b, 0), (a, 1), (b, 1)]
    attend_rows(q, 0, every, o, lse)
    attend_rows(q, 1, every[2:], o, lse)
    left, terms = lse[...], []
    for _ in range(3):
        terms.append(left.astype(jnp.bfloat16))
        left = left - terms[-1].astype(jnp.float32)
    terms.append(jnp.zeros_like(terms[0]))
    last = 2 * q.shape[2]
    o[0, pl.ds(last, 4 * lse.shape[0])] = jnp.concatenate(
        [term.astype(jnp.float32) for term in terms], axis=0
    ).astype(jnp.bfloat16)


def near_kernel(count, q, ka, va, kb, vb, *rest):
    o, lse = rest[count:]
    a, b = (ka, va), (kb, vb)
    own = [(a, 0), (b, 0), (a, 1), (b, 1)]
    attend_rows(q, 0, own[:2], o, lse.at[0])
    attend_rows(q, 1, own, o, lse.at[0])


def blend(first, first_lse, other, other_lse, usable, store):
    share = jnp.where(usable, 1.0, 0.0) / (1.0 + jnp.exp2(first_lse - other_lse))
    for row in range(first.shape[1] // TILE):
        at = pl.ds(row * TILE, TILE)
        weight = jnp.broadcast_to(share[row : row + 1], (HEAD_DIM, TILE)).T
        start = first[0, at]
        store(at, start + weight * (other[0, at].astype(jnp.float32) - start))
    more = jnp.log2(1.0 + jnp.exp2(-jnp.abs(first_lse - other_lse)))
    return jnp.where(usable, jnp.maximum(first_lse, other_lse) + more, first_lse)


def far_kernel(count, meta, q, ka, va, kb, vb, o_near, lse_near, *rest):
    o, lse, part, part_lse = rest[count:]
    a, b = (ka, va), (kb, vb)
    every = [(a, 0), (b, 0), (a, 1), (b, 1)]

    def store(at, block):
        o[0, at] = block

    @pl.when(meta[8] >= 1)
    def _():
        attend_rows(q, 0, every, part, part_lse)
        attend_rows(q, 1, every, part, part_lse)
        lse[0] = blend(o_near, lse_near[0], part, part_lse[...], True, store)

    @pl.when(meta[8] < 1)
    def _():
        o[...] = o_near[...]
        lse[...] = lse_near[...]


def in_order_kernel(*refs):
    pass


def in_order(blocks, after):
    return pl.pallas_call(
        in_order_kernel,
        out_shape=[jax.ShapeDtypeStruct(block.shape, block.dtype) for block in blocks],
        in_specs=[ANY] * (len(blocks) + len(after)),
        out_specs=[ANY] * len(blocks),
        input_output_aliases={n: n for n in range(len(blocks))},
        compiler_params=params(1),
        cost_estimate=pl.CostEstimate(flops=0, bytes_accessed=0, transcendentals=0),
        name="in_order",
    )(*blocks, *after)


def halves_kernel(count, kv, *rest):
    k, v, sems = rest[count:]
    heads = k.shape[0]
    copies = [
        pltpu.make_async_copy(kv.at[pl.ds(n * heads, heads)], out, sems.at[n])
        for n, out in enumerate((k, v))
    ]
    for copy in copies:
        copy.start()
    for copy in copies:
        copy.wait()


def halves(kv, after):
    half = jax.ShapeDtypeStruct((kv.shape[0] // 2,) + kv.shape[1:], kv.dtype)
    return pl.pallas_call(
        functools.partial(halves_kernel, len(after)),
        out_shape=[half, half],
        in_specs=[ANY] * (1 + len(after)),
        out_specs=[ANY] * 2,
        scratch_shapes=[pltpu.SemaphoreType.DMA((2,))],
        compiler_params=params(1),
        cost_estimate=estimate(0),
        name="halves",
    )(kv, *after)


def lse_rows(rows):
    return -(-2 * rows // TILE // 8) * 8


def attend(body, meta, q, kv, near, after, cost):
    heads, _, rows, _ = q.shape
    block = (1, 2, rows, HEAD_DIM)
    head = pl.BlockSpec(block, lambda h: (h, 0, 0, 0))
    value = pl.BlockSpec(block, lambda h: (heads + h, 0, 0, 0))
    extra = lse_rows(rows)
    by_head = lambda h: (h, 0, 0)
    o_spec = pl.BlockSpec((1, 2 * rows, HEAD_DIM), by_head)
    lse_spec = pl.BlockSpec((1, extra, TILE), by_head)
    part_lse = pltpu.VMEM((extra, TILE), jnp.float32)
    operands, specs = [q], [head]
    for half in kv:
        apart = isinstance(half, tuple)
        operands += half if apart else [half, half]
        specs += [head, head if apart else value]
    out_shape = [
        jax.ShapeDtypeStruct((heads, 2 * rows, HEAD_DIM), jnp.float32),
        jax.ShapeDtypeStruct((heads, extra, TILE), jnp.float32),
    ]
    out_specs, scratch = [o_spec, lse_spec], []
    if body is remote_kernel:
        length = 2 * rows + 4 * extra
        out_shape = jax.ShapeDtypeStruct((heads, length, HEAD_DIM), jnp.bfloat16)
        out_specs = pl.BlockSpec((1, length, HEAD_DIM), by_head)
        scratch = [part_lse]
    if body is far_kernel:
        operands = [meta] + operands + list(near)
        specs = [SMEM] + specs + [o_spec, lse_spec]
        scratch = [pltpu.VMEM((1, 2 * rows, HEAD_DIM), jnp.float32), part_lse]
    return pl.pallas_call(
        functools.partial(body, len(after)),
        grid=(heads,),
        out_shape=out_shape,
        in_specs=specs + [ANY] * len(after),
        out_specs=out_specs,
        scratch_shapes=scratch,
        compiler_params=params(20),
        cost_estimate=estimate(cost),
        name=body.__name__[:-7],
    )(*operands, *after)


def merge_kernel(count, meta, o, lse, o_far, *rest):
    outs, scratch = rest[count : count + 4], rest[count + 4]
    rows = o.shape[1] // 2
    half = rows // 2
    extra = lse.shape[1]
    terms = o_far[0, pl.ds(2 * rows, 4 * extra)].astype(jnp.float32)
    lse_far = terms[:extra] + terms[extra : 2 * extra] + terms[2 * extra : 3 * extra]

    def store(at, block):
        scratch[at] = block

    blend(o, lse[0], o_far, lse_far, meta[8] >= 2, store)
    for j, (dx, _) in enumerate(PLACES):
        at = pl.ds(pl.multiple_of(meta[4 + j] * rows + dx * half, half), half)
        outs[j][0] = scratch[at].astype(outs[j].dtype)


def merge(meta, o, lse, o_far, after, cost):
    heads, both, _ = o.shape
    by_head = lambda h: (h, 0, 0)
    return pl.pallas_call(
        functools.partial(merge_kernel, len(after)),
        grid=(heads,),
        out_shape=[jax.ShapeDtypeStruct((heads, both // 4, HEAD_DIM), jnp.bfloat16)] * 4,
        in_specs=[SMEM]
        + [pl.BlockSpec((1,) + a.shape[1:], by_head) for a in (o, lse, o_far)]
        + [ANY] * len(after),
        out_specs=[pl.BlockSpec((1, both // 4, HEAD_DIM), by_head)] * 4,
        scratch_shapes=[pltpu.VMEM((both, HEAD_DIM), jnp.float32)],
        compiler_params=params(12),
        cost_estimate=estimate(cost),
        name="merge",
    )(meta, o, lse, o_far, *after)


def finish_kernel(firsts, group_width, meta, gate, *refs):
    pieces, out = refs[:-1], refs[-1]
    for i, piece in enumerate(pieces):
        chunk, j = divmod(i, 4)
        for h in range(piece.shape[0]):
            column = meta[j] * group_width + (firsts[chunk] + h) * HEAD_DIM
            at = pl.ds(pl.multiple_of(column, HEAD_DIM), HEAD_DIM)
            out[:, at] = (gate[:, at] * piece[h].astype(jnp.float32)).astype(out.dtype)


def finish(meta, gate, pieces, firsts, group_width, cost=0):
    rows = pieces[0].shape[1]
    whole = pl.BlockSpec(memory_space=pltpu.VMEM)
    return pl.pallas_call(
        functools.partial(finish_kernel, firsts, group_width),
        out_shape=jax.ShapeDtypeStruct((rows, 4 * group_width), jnp.bfloat16),
        in_specs=[SMEM] + [whole] * (1 + len(pieces)),
        out_specs=whole,
        compiler_params=params(16),
        cost_estimate=estimate(cost),
        name="finish",
    )(meta, gate, *pieces)


def chunk_sizes(heads):
    sizes = []
    for size in SIZES:
        if sum(sizes) + size <= heads:
            sizes.append(size)
    return sizes + [1] * (heads - sum(sizes))


def shards(queries, keys, values, level_index, plan, gate_weight):
    span = lax.axis_index("span")
    member = lax.axis_index("seq")
    x, y = member // 2, span % 2
    group_width = queries.shape[1] // 4
    group_heads = group_width // HEAD_DIM
    meta = jnp.stack(
        [2 * (x ^ dx) + (y ^ dy) for dx, dy in PLACES]
        + [y ^ dy for _, dy in PLACES]
        + [span // 2]
    ).astype(jnp.int32)
    gate = timestep_gate(level_index, plan, gate_weight, span)

    sizes = chunk_sizes(group_heads)
    firsts = [sum(sizes[:i]) for i in range(len(sizes))]
    chunks = range(len(sizes))

    sent = pack(meta, queries, keys, values, firsts, sizes, group_width)
    last = [gate]

    q, kv, kv_up, q_down = {}, {}, {}, {}
    far, own, results = {}, {}, {}

    def exchange(blocks):
        return [blocks[0]] + [move(blocks[j], within_level(*PLACES[j])) for j in (1, 2, 3)]

    exchanged = {0: exchange(sent[0])}
    if EARLY and len(sizes) > 1:
        exchanged[1] = exchange([sent[1][0], *in_order(sent[1][1:], last)])

    def spread(i, after, cost):
        pieces = exchanged.pop(i)
        later = sent[i + 1] if i + 1 < len(sizes) and i + 1 not in exchanged else []
        q[i], kv[i], later = stack(meta, pieces, later[1:], after, cost)
        if later:
            exchanged[i + 1] = exchange([sent[i + 1][0], *later])
        kv_up[i] = move(kv[i], one_up)
        q_down[i] = move(q[i], one_down)
        kv[i] = (kv[i], move(kv[i], other_core))
        return [q[i]]

    def near(i, after, cost):
        own[i] = attend(near_kernel, meta, q[i], kv[i], None, after, cost)
        return [own[i][1]]

    def remote(i, after, cost):
        if i in APART:
            held = tuple(halves(kv_up[i], after))
            kv_up[i] = (held, tuple(move(half, other_core) for half in held))
        else:
            held = in_order([kv_up[i]], after)[0]
            kv_up[i] = (held, move(held, other_core))
        part = attend(remote_kernel, meta, q_down[i], kv_up[i], None, [], cost)
        far[i] = move(part, one_up)
        return [part]

    def own_far(i, after, cost):
        own[i] = attend(far_kernel, meta, q[i], kv_up[i], own[i], after, cost)
        return [own[i][1]]

    def close(i, after, cost):
        merged = merge(meta, *own[i], far[i], after, cost)
        results[i] = exchange(merged)
        return [merged[0]]

    steps = {"s": spread, "n": near, "r": remote, "f": own_far, "c": close}
    for step in ORDER.split():
        name, *extra = step.split("+")
        extra = [{"q": q_down, "o": far}[e[0]][int(e[1])] for e in extra]
        last = steps[name[0]](int(name[1]), last + extra, COSTS.get(name, 0))
    return finish(meta, gate, sum((results[i] for i in chunks), []), firsts, group_width)


def solution(mesh):
    rows = P(AXES, None)
    return jax.shard_map(
        shards,
        mesh=mesh,
        in_specs=(rows, rows, rows, P(), P(), P()),
        out_specs=rows,
        check_vma=False,
    )
```

```python
import functools
import math

import jax
import jax.numpy as jnp
from jax import lax
from jax.experimental import pallas as pl
from jax.experimental.pallas import tpu as pltpu
from jax.sharding import PartitionSpec as P

HEAD_DIM = 128
AXES = ("span", "seq")
ANY = pl.BlockSpec(memory_space=pl.ANY)
SMEM = pl.BlockSpec(memory_space=pltpu.SMEM)
MIB = 1024 * 1024
TILE = 128
SIZES = (3, 2)
APART = (0,)
COSTS = {}
EARLY = False
ORDER = "s0 n0 s1+q0 r0 n1+q1 r1 f0 f1 c0 c1"
NT = (((1,), (1,)), ((), ()))
NN = (((1,), (0,)), ((), ()))


def params(mib):
    return pltpu.CompilerParams(vmem_limit_bytes=mib * MIB)


def estimate(microseconds):
    return pl.CostEstimate(
        flops=0, bytes_accessed=int(microseconds * 3.6e6) + 1000, transcendentals=0
    )


def move(block, target):
    spans, members = lax.axis_size("span"), lax.axis_size("seq")
    route = []
    for device in range(spans * members):
        span, member = divmod(device, members)
        to_span, to_member = target(span, member)
        if 0 <= to_span < spans:
            route.append((device, to_span * members + to_member))
    return lax.ppermute(block, AXES, route)


def within_level(dx, dy):
    return lambda span, member: (span ^ dy, member ^ (2 * dx))


def other_core(span, member):
    return span, member ^ 1


def one_up(span, member):
    return span + 2, member


def one_down(span, member):
    return span - 2, member


PLACES = ((0, 0), (0, 1), (1, 0), (1, 1))


def timestep_gate(level_index, plan, gate_weight, span_number):
    noise_level = jnp.sum(
        jnp.where(jnp.arange(level_index.shape[0], dtype=jnp.int32) == span_number, level_index, 0)
    )
    timestep = jnp.sum(
        jnp.where(jnp.arange(plan.shape[0], dtype=jnp.int32) == noise_level, plan, 0)
    )
    half_freq = gate_weight.shape[0] // 2
    frequencies = jnp.exp(-math.log(10000.0) * jnp.arange(half_freq, dtype=jnp.float32) / half_freq)
    angles = timestep.astype(jnp.float32) * frequencies
    embedding = jnp.concatenate([jnp.cos(angles), jnp.sin(angles)])[None, :]
    return jnp.dot(
        embedding, gate_weight, precision=lax.Precision.HIGHEST, preferred_element_type=jnp.float32
    )


def pack_kernel(first, heads, group_width, count, meta, q, k, v, *rest):
    outs = rest[count:]
    for j in range(4):
        for t, ref in enumerate((q, k, v)):
            for h in range(heads):
                column = meta[j] * group_width + (first + h) * HEAD_DIM
                at = pl.ds(pl.multiple_of(column, HEAD_DIM), HEAD_DIM)
                outs[j][t * heads + h] = ref[:, at]


def pack(meta, q, k, v, first, heads, group_width, after):
    rows = q.shape[0]
    whole = pl.BlockSpec(memory_space=pltpu.VMEM)
    return pl.pallas_call(
        functools.partial(pack_kernel, first, heads, group_width, len(after)),
        out_shape=[jax.ShapeDtypeStruct((3 * heads, rows, HEAD_DIM), q.dtype)] * 4,
        in_specs=[SMEM, whole, whole, whole] + [ANY] * len(after),
        out_specs=[whole] * 4,
        compiler_params=params(60),
        cost_estimate=estimate(0),
        name="pack",
    )(meta, q, k, v, *after)


def stack_kernel(heads, count, meta, *refs):
    pieces, outs = refs[:4], refs[4 + count :]
    (q_out, kv_out), sems = outs[:2], outs[-1]
    rows = pieces[0].shape[1]
    copies = []
    for j, (dx, _) in enumerate(PLACES):
        parity = meta[4 + j]
        at = pl.ds(dx * rows, rows)
        for t, (source, target) in enumerate(
            (
                (pieces[j].at[pl.ds(heads, 2 * heads)], kv_out.at[:, parity, at]),
                (pieces[j].at[pl.ds(0, heads)], q_out.at[:, parity, at]),
            )
        ):
            copy = pltpu.make_async_copy(source, target, sems.at[j, t])
            copy.start()
            copies.append(copy)
    for copy in copies:
        copy.wait()


def stack(meta, pieces, later, after, cost):
    triple, rows, _ = pieces[0].shape
    heads = triple // 3
    dtype = pieces[0].dtype
    outs = pl.pallas_call(
        functools.partial(stack_kernel, heads, len(later) + len(after)),
        out_shape=[
            jax.ShapeDtypeStruct((heads, 2, 2 * rows, HEAD_DIM), dtype),
            jax.ShapeDtypeStruct((2 * heads, 2, 2 * rows, HEAD_DIM), dtype),
        ]
        + [jax.ShapeDtypeStruct(block.shape, block.dtype) for block in later],
        in_specs=[SMEM] + [ANY] * (4 + len(later) + len(after)),
        out_specs=[ANY] * (2 + len(later)),
        scratch_shapes=[pltpu.SemaphoreType.DMA((4, 2))],
        input_output_aliases={5 + n: 2 + n for n in range(len(later))},
        compiler_params=params(8),
        cost_estimate=estimate(cost),
        name="stack",
    )(meta, *pieces, *later, *after)
    return outs[0], outs[1], outs[2:]


def softmax_part(q, keys, values):
    scale = math.log2(math.e) / math.sqrt(HEAD_DIM)
    scores = [lax.dot_general(q, k, NT, preferred_element_type=jnp.float32) for k in keys]
    peak = functools.reduce(jnp.maximum, scores).max(axis=1, keepdims=True)
    peak = peak * scale
    weights = [jnp.exp2(s * scale - peak) for s in scores]
    total = functools.reduce(jnp.add, weights).sum(axis=1, keepdims=True)
    out = functools.reduce(
        jnp.add,
        [
            lax.dot_general(w.astype(jnp.bfloat16), v, NN, preferred_element_type=jnp.float32)
            for w, v in zip(weights, values)
        ],
    )
    return out / total, peak + jnp.log2(total)


def attend_rows(q_ref, p, blocks, o_ref, lse_ref):
    rows, q = q_ref.shape[2], q_ref[0, p or 0]
    if p is None:
        rows, p, q = 2 * rows, 0, q_ref[0].reshape(2 * rows, HEAD_DIM)
    out, lse = softmax_part(
        q, [kv[0][0, i] for kv, i in blocks], [kv[1][0, i] for kv, i in blocks]
    )
    o_ref[0, pl.ds(p * rows, rows)] = out.astype(o_ref.dtype)
    for t in range(rows // TILE):
        column = jnp.broadcast_to(lse[t * TILE : (t + 1) * TILE], (TILE, TILE))
        lse_ref[pl.ds(p * (rows // TILE) + t, 1)] = column.T[:1]


def remote_kernel(count, q, ka, va, kb, vb, *rest):
    o, lse = rest[count:]
    a, b = (ka, va), (kb, vb)
    every = [(a, 0), (b, 0), (a, 1), (b, 1)]
    attend_rows(q, 0, every, o, lse)
    attend_rows(q, 1, every[2:], o, lse)
    left, terms = lse[...], []
    for _ in range(3):
        terms.append(left.astype(jnp.bfloat16))
        left = left - terms[-1].astype(jnp.float32)
    terms.append(jnp.zeros_like(terms[0]))
    last = 2 * q.shape[2]
    o[0, pl.ds(last, 4 * lse.shape[0])] = jnp.concatenate(
        [term.astype(jnp.float32) for term in terms], axis=0
    ).astype(jnp.bfloat16)


def near_kernel(count, q, ka, va, kb, vb, *rest):
    o, lse = rest[count:]
    a, b = (ka, va), (kb, vb)
    own = [(a, 0), (b, 0), (a, 1), (b, 1)]
    attend_rows(q, 0, own[:2], o, lse.at[0])
    attend_rows(q, 1, own, o, lse.at[0])


def blend(first, first_lse, other, other_lse, usable, store):
    share = jnp.where(usable, 1.0, 0.0) / (1.0 + jnp.exp2(first_lse - other_lse))
    for row in range(first.shape[1] // TILE):
        at = pl.ds(row * TILE, TILE)
        weight = jnp.broadcast_to(share[row : row + 1], (HEAD_DIM, TILE)).T
        start = first[0, at]
        store(at, start + weight * (other[0, at].astype(jnp.float32) - start))
    more = jnp.log2(1.0 + jnp.exp2(-jnp.abs(first_lse - other_lse)))
    return jnp.where(usable, jnp.maximum(first_lse, other_lse) + more, first_lse)


def far_kernel(count, meta, q, ka, va, kb, vb, o_near, lse_near, *rest):
    o, lse, part, part_lse = rest[count:]
    a, b = (ka, va), (kb, vb)
    every = [(a, 0), (b, 0), (a, 1), (b, 1)]

    def store(at, block):
        o[0, at] = block

    @pl.when(meta[8] >= 1)
    def _():
        attend_rows(q, None, every, part, part_lse)
        lse[0] = blend(o_near, lse_near[0], part, part_lse[...], True, store)

    @pl.when(meta[8] < 1)
    def _():
        o[...] = o_near[...]
        lse[...] = lse_near[...]


def in_order_kernel(*refs):
    pass


def in_order(blocks, after):
    return pl.pallas_call(
        in_order_kernel,
        out_shape=[jax.ShapeDtypeStruct(block.shape, block.dtype) for block in blocks],
        in_specs=[ANY] * (len(blocks) + len(after)),
        out_specs=[ANY] * len(blocks),
        input_output_aliases={n: n for n in range(len(blocks))},
        compiler_params=params(1),
        cost_estimate=pl.CostEstimate(flops=0, bytes_accessed=0, transcendentals=0),
        name="in_order",
    )(*blocks, *after)


def halves_kernel(count, kv, *rest):
    k, v, sems = rest[count:]
    heads = k.shape[0]
    copies = [
        pltpu.make_async_copy(kv.at[pl.ds(n * heads, heads)], out, sems.at[n])
        for n, out in enumerate((k, v))
    ]
    for copy in copies:
        copy.start()
    for copy in copies:
        copy.wait()


def halves(kv, after):
    half = jax.ShapeDtypeStruct((kv.shape[0] // 2,) + kv.shape[1:], kv.dtype)
    return pl.pallas_call(
        functools.partial(halves_kernel, len(after)),
        out_shape=[half, half],
        in_specs=[ANY] * (1 + len(after)),
        out_specs=[ANY] * 2,
        scratch_shapes=[pltpu.SemaphoreType.DMA((2,))],
        compiler_params=params(1),
        cost_estimate=estimate(0),
        name="halves",
    )(kv, *after)


def lse_rows(rows):
    return -(-2 * rows // TILE // 8) * 8


def attend(body, meta, q, kv, near, after, cost):
    heads, _, rows, _ = q.shape
    block = (1, 2, rows, HEAD_DIM)
    head = pl.BlockSpec(block, lambda h: (h, 0, 0, 0))
    value = pl.BlockSpec(block, lambda h: (heads + h, 0, 0, 0))
    extra = lse_rows(rows)
    by_head = lambda h: (h, 0, 0)
    o_spec = pl.BlockSpec((1, 2 * rows, HEAD_DIM), by_head)
    lse_spec = pl.BlockSpec((1, extra, TILE), by_head)
    part_lse = pltpu.VMEM((extra, TILE), jnp.float32)
    operands, specs = [q], [head]
    for half in kv:
        apart = isinstance(half, tuple)
        operands += half if apart else [half, half]
        specs += [head, head if apart else value]
    out_shape = [
        jax.ShapeDtypeStruct((heads, 2 * rows, HEAD_DIM), jnp.float32),
        jax.ShapeDtypeStruct((heads, extra, TILE), jnp.float32),
    ]
    out_specs, scratch = [o_spec, lse_spec], []
    if body is remote_kernel:
        length = 2 * rows + 4 * extra
        out_shape = jax.ShapeDtypeStruct((heads, length, HEAD_DIM), jnp.bfloat16)
        out_specs = pl.BlockSpec((1, length, HEAD_DIM), by_head)
        scratch = [part_lse]
    if body is far_kernel:
        operands = [meta] + operands + list(near)
        specs = [SMEM] + specs + [o_spec, lse_spec]
        scratch = [pltpu.VMEM((1, 2 * rows, HEAD_DIM), jnp.float32), part_lse]
    return pl.pallas_call(
        functools.partial(body, len(after)),
        grid=(heads,),
        out_shape=out_shape,
        in_specs=specs + [ANY] * len(after),
        out_specs=out_specs,
        scratch_shapes=scratch,
        compiler_params=params(20),
        cost_estimate=estimate(cost),
        name=body.__name__[:-7],
    )(*operands, *after)


def merge_kernel(count, meta, o, lse, o_far, *rest):
    outs, scratch = rest[count : count + 4], rest[count + 4]
    rows = o.shape[1] // 2
    half = rows // 2
    extra = lse.shape[1]
    terms = o_far[0, pl.ds(2 * rows, 4 * extra)].astype(jnp.float32)
    lse_far = terms[:extra] + terms[extra : 2 * extra] + terms[2 * extra : 3 * extra]

    def store(at, block):
        scratch[at] = block

    blend(o, lse[0], o_far, lse_far, meta[8] >= 2, store)
    for j, (dx, _) in enumerate(PLACES):
        at = pl.ds(pl.multiple_of(meta[4 + j] * rows + dx * half, half), half)
        outs[j][0] = scratch[at].astype(outs[j].dtype)


def merge(meta, o, lse, o_far, after, cost):
    heads, both, _ = o.shape
    by_head = lambda h: (h, 0, 0)
    return pl.pallas_call(
        functools.partial(merge_kernel, len(after)),
        grid=(heads,),
        out_shape=[jax.ShapeDtypeStruct((heads, both // 4, HEAD_DIM), jnp.bfloat16)] * 4,
        in_specs=[SMEM]
        + [pl.BlockSpec((1,) + a.shape[1:], by_head) for a in (o, lse, o_far)]
        + [ANY] * len(after),
        out_specs=[pl.BlockSpec((1, both // 4, HEAD_DIM), by_head)] * 4,
        scratch_shapes=[pltpu.VMEM((both, HEAD_DIM), jnp.float32)],
        compiler_params=params(12),
        cost_estimate=estimate(cost),
        name="merge",
    )(meta, o, lse, o_far, *after)


def finish_kernel(firsts, group_width, meta, gate, *refs):
    pieces, out = refs[:-1], refs[-1]
    for i, piece in enumerate(pieces):
        chunk, j = divmod(i, 4)
        for h in range(piece.shape[0]):
            column = meta[j] * group_width + (firsts[chunk] + h) * HEAD_DIM
            at = pl.ds(pl.multiple_of(column, HEAD_DIM), HEAD_DIM)
            out[:, at] = (gate[:, at] * piece[h].astype(jnp.float32)).astype(out.dtype)


def finish(meta, gate, pieces, firsts, group_width, cost=0):
    rows = pieces[0].shape[1]
    whole = pl.BlockSpec(memory_space=pltpu.VMEM)
    return pl.pallas_call(
        functools.partial(finish_kernel, firsts, group_width),
        out_shape=jax.ShapeDtypeStruct((rows, 4 * group_width), jnp.bfloat16),
        in_specs=[SMEM] + [whole] * (1 + len(pieces)),
        out_specs=whole,
        compiler_params=params(16),
        cost_estimate=estimate(cost),
        name="finish",
    )(meta, gate, *pieces)


def chunk_sizes(heads):
    sizes = []
    for size in SIZES:
        if sum(sizes) + size <= heads:
            sizes.append(size)
    return sizes + [1] * (heads - sum(sizes))


def shards(queries, keys, values, level_index, plan, gate_weight):
    span = lax.axis_index("span")
    member = lax.axis_index("seq")
    x, y = member // 2, span % 2
    group_width = queries.shape[1] // 4
    group_heads = group_width // HEAD_DIM
    meta = jnp.stack(
        [2 * (x ^ dx) + (y ^ dy) for dx, dy in PLACES]
        + [y ^ dy for _, dy in PLACES]
        + [span // 2]
    ).astype(jnp.int32)
    gate = timestep_gate(level_index, plan, gate_weight, span)

    sizes = chunk_sizes(group_heads)
    firsts = [sum(sizes[:i]) for i in range(len(sizes))]
    chunks = range(len(sizes))

    sent, packed = [], []
    for first, size in zip(firsts, sizes):
        sent.append(pack(meta, queries, keys, values, first, size, group_width, packed))
        packed = [sent[-1][0]]
    last = [gate]

    q, kv, kv_up, q_down = {}, {}, {}, {}
    far, own, results = {}, {}, {}

    def exchange(blocks):
        return [blocks[0]] + [move(blocks[j], within_level(*PLACES[j])) for j in (1, 2, 3)]

    exchanged = {0: exchange(sent[0])}
    if EARLY and len(sizes) > 1:
        exchanged[1] = exchange([sent[1][0], *in_order(sent[1][1:], last)])

    def spread(i, after, cost):
        pieces = exchanged.pop(i)
        later = sent[i + 1] if i + 1 < len(sizes) and i + 1 not in exchanged else []
        q[i], kv[i], later = stack(meta, pieces, later[1:], after, cost)
        if later:
            exchanged[i + 1] = exchange([sent[i + 1][0], *later])
        kv_up[i] = move(kv[i], one_up)
        q_down[i] = move(q[i], one_down)
        kv[i] = (kv[i], move(kv[i], other_core))
        return [q[i]]

    def near(i, after, cost):
        own[i] = attend(near_kernel, meta, q[i], kv[i], None, after, cost)
        return [own[i][1]]

    def remote(i, after, cost):
        if i in APART:
            held = tuple(halves(kv_up[i], after))
            kv_up[i] = (held, tuple(move(half, other_core) for half in held))
        else:
            held = in_order([kv_up[i]], after)[0]
            kv_up[i] = (held, move(held, other_core))
        part = attend(remote_kernel, meta, q_down[i], kv_up[i], None, [], cost)
        far[i] = move(part, one_up)
        return [part]

    def own_far(i, after, cost):
        own[i] = attend(far_kernel, meta, q[i], kv_up[i], own[i], after, cost)
        return [own[i][1]]

    def close(i, after, cost):
        merged = merge(meta, *own[i], far[i], after, cost)
        results[i] = exchange(merged)
        return [merged[0]]

    steps = {"s": spread, "n": near, "r": remote, "f": own_far, "c": close}
    for step in ORDER.split():
        name, *extra = step.split("+")
        extra = [{"q": q_down, "o": far}[e[0]][int(e[1])] for e in extra]
        last = steps[name[0]](int(name[1]), last + extra, COSTS.get(name, 0))
    return finish(meta, gate, sum((results[i] for i in chunks), []), firsts, group_width)


def solution(mesh):
    rows = P(AXES, None)
    return jax.shard_map(
        shards,
        mesh=mesh,
        in_specs=(rows, rows, rows, P(), P(), P()),
        out_specs=rows,
        check_vma=False,
    )
```

```python
import functools
import math

import jax
import jax.numpy as jnp
from jax import lax
from jax.experimental import pallas as pl
from jax.experimental.pallas import tpu as pltpu
from jax.sharding import PartitionSpec as P

HEAD_DIM = 128
AXES = ("span", "seq")
ANY = pl.BlockSpec(memory_space=pl.ANY)
SMEM = pl.BlockSpec(memory_space=pltpu.SMEM)
MIB = 1024 * 1024
TILE = 128
SIZES = (3, 2)
APART = (0,)
COSTS = {}
EARLY = False
ORDER = "s0 n0 s1+q0 r0 f0 r1+q1 n1 f1 c0 c1"
NT = (((1,), (1,)), ((), ()))
NN = (((1,), (0,)), ((), ()))


def params(mib):
    return pltpu.CompilerParams(vmem_limit_bytes=mib * MIB)


def estimate(microseconds):
    return pl.CostEstimate(
        flops=0, bytes_accessed=int(microseconds * 3.6e6) + 1000, transcendentals=0
    )


def move(block, target):
    spans, members = lax.axis_size("span"), lax.axis_size("seq")
    route = []
    for device in range(spans * members):
        span, member = divmod(device, members)
        to_span, to_member = target(span, member)
        if 0 <= to_span < spans:
            route.append((device, to_span * members + to_member))
    return lax.ppermute(block, AXES, route)


def within_level(dx, dy):
    return lambda span, member: (span ^ dy, member ^ (2 * dx))


def other_core(span, member):
    return span, member ^ 1


def one_up(span, member):
    return span + 2, member


def one_down(span, member):
    return span - 2, member


PLACES = ((0, 0), (0, 1), (1, 0), (1, 1))


def timestep_gate(level_index, plan, gate_weight, span_number):
    noise_level = jnp.sum(
        jnp.where(jnp.arange(level_index.shape[0], dtype=jnp.int32) == span_number, level_index, 0)
    )
    timestep = jnp.sum(
        jnp.where(jnp.arange(plan.shape[0], dtype=jnp.int32) == noise_level, plan, 0)
    )
    half_freq = gate_weight.shape[0] // 2
    frequencies = jnp.exp(-math.log(10000.0) * jnp.arange(half_freq, dtype=jnp.float32) / half_freq)
    angles = timestep.astype(jnp.float32) * frequencies
    embedding = jnp.concatenate([jnp.cos(angles), jnp.sin(angles)])[None, :]
    return jnp.dot(
        embedding, gate_weight, precision=lax.Precision.HIGHEST, preferred_element_type=jnp.float32
    )


def pack_kernel(first, heads, group_width, count, meta, q, k, v, *rest):
    outs = rest[count:]
    for j in range(4):
        for t, ref in enumerate((q, k, v)):
            for h in range(heads):
                column = meta[j] * group_width + (first + h) * HEAD_DIM
                at = pl.ds(pl.multiple_of(column, HEAD_DIM), HEAD_DIM)
                outs[j][t * heads + h] = ref[:, at]


def pack(meta, q, k, v, first, heads, group_width, after):
    rows = q.shape[0]
    whole = pl.BlockSpec(memory_space=pltpu.VMEM)
    return pl.pallas_call(
        functools.partial(pack_kernel, first, heads, group_width, len(after)),
        out_shape=[jax.ShapeDtypeStruct((3 * heads, rows, HEAD_DIM), q.dtype)] * 4,
        in_specs=[SMEM, whole, whole, whole] + [ANY] * len(after),
        out_specs=[whole] * 4,
        compiler_params=params(60),
        cost_estimate=estimate(0),
        name="pack",
    )(meta, q, k, v, *after)


def stack_kernel(heads, count, meta, *refs):
    pieces, outs = refs[:4], refs[4 + count :]
    (q_out, kv_out), sems = outs[:2], outs[-1]
    rows = pieces[0].shape[1]
    copies = []
    for j, (dx, _) in enumerate(PLACES):
        parity = meta[4 + j]
        at = pl.ds(dx * rows, rows)
        for t, (source, target) in enumerate(
            (
                (pieces[j].at[pl.ds(heads, 2 * heads)], kv_out.at[:, parity, at]),
                (pieces[j].at[pl.ds(0, heads)], q_out.at[:, parity, at]),
            )
        ):
            copy = pltpu.make_async_copy(source, target, sems.at[j, t])
            copy.start()
            copies.append(copy)
    for copy in copies:
        copy.wait()


def stack(meta, pieces, later, after, cost):
    triple, rows, _ = pieces[0].shape
    heads = triple // 3
    dtype = pieces[0].dtype
    outs = pl.pallas_call(
        functools.partial(stack_kernel, heads, len(later) + len(after)),
        out_shape=[
            jax.ShapeDtypeStruct((heads, 2, 2 * rows, HEAD_DIM), dtype),
            jax.ShapeDtypeStruct((2 * heads, 2, 2 * rows, HEAD_DIM), dtype),
        ]
        + [jax.ShapeDtypeStruct(block.shape, block.dtype) for block in later],
        in_specs=[SMEM] + [ANY] * (4 + len(later) + len(after)),
        out_specs=[ANY] * (2 + len(later)),
        scratch_shapes=[pltpu.SemaphoreType.DMA((4, 2))],
        input_output_aliases={5 + n: 2 + n for n in range(len(later))},
        compiler_params=params(8),
        cost_estimate=estimate(cost),
        name="stack",
    )(meta, *pieces, *later, *after)
    return outs[0], outs[1], outs[2:]


def softmax_part(q, keys, values):
    scale = math.log2(math.e) / math.sqrt(HEAD_DIM)
    scores = [lax.dot_general(q, k, NT, preferred_element_type=jnp.float32) for k in keys]
    peak = functools.reduce(jnp.maximum, scores).max(axis=1, keepdims=True)
    peak = peak * scale
    weights = [jnp.exp2(s * scale - peak) for s in scores]
    total = functools.reduce(jnp.add, weights).sum(axis=1, keepdims=True)
    out = functools.reduce(
        jnp.add,
        [
            lax.dot_general(w.astype(jnp.bfloat16), v, NN, preferred_element_type=jnp.float32)
            for w, v in zip(weights, values)
        ],
    )
    return out / total, peak + jnp.log2(total)


def attend_rows(q_ref, p, blocks, o_ref, lse_ref):
    rows, q = q_ref.shape[2], q_ref[0, p or 0]
    if p is None:
        rows, p, q = 2 * rows, 0, q_ref[0].reshape(2 * rows, HEAD_DIM)
    out, lse = softmax_part(
        q, [kv[0][0, i] for kv, i in blocks], [kv[1][0, i] for kv, i in blocks]
    )
    o_ref[0, pl.ds(p * rows, rows)] = out.astype(o_ref.dtype)
    for t in range(rows // TILE):
        column = jnp.broadcast_to(lse[t * TILE : (t + 1) * TILE], (TILE, TILE))
        lse_ref[pl.ds(p * (rows // TILE) + t, 1)] = column.T[:1]


def remote_kernel(count, q, ka, va, kb, vb, *rest):
    o, lse = rest[count:]
    a, b = (ka, va), (kb, vb)
    every = [(a, 0), (b, 0), (a, 1), (b, 1)]
    attend_rows(q, 0, every, o, lse)
    attend_rows(q, 1, every[2:], o, lse)
    left, terms = lse[...], []
    for _ in range(3):
        terms.append(left.astype(jnp.bfloat16))
        left = left - terms[-1].astype(jnp.float32)
    terms.append(jnp.zeros_like(terms[0]))
    last = 2 * q.shape[2]
    o[0, pl.ds(last, 4 * lse.shape[0])] = jnp.concatenate(
        [term.astype(jnp.float32) for term in terms], axis=0
    ).astype(jnp.bfloat16)


def near_kernel(count, q, ka, va, kb, vb, *rest):
    o, lse = rest[count:]
    a, b = (ka, va), (kb, vb)
    own = [(a, 0), (b, 0), (a, 1), (b, 1)]
    attend_rows(q, 0, own[:2], o, lse.at[0])
    attend_rows(q, 1, own, o, lse.at[0])


def blend(first, first_lse, other, other_lse, usable, store):
    share = jnp.where(usable, 1.0, 0.0) / (1.0 + jnp.exp2(first_lse - other_lse))
    for row in range(first.shape[1] // TILE):
        at = pl.ds(row * TILE, TILE)
        weight = jnp.broadcast_to(share[row : row + 1], (HEAD_DIM, TILE)).T
        start = first[0, at]
        store(at, start + weight * (other[0, at].astype(jnp.float32) - start))
    more = jnp.log2(1.0 + jnp.exp2(-jnp.abs(first_lse - other_lse)))
    return jnp.where(usable, jnp.maximum(first_lse, other_lse) + more, first_lse)


def far_kernel(count, meta, q, ka, va, kb, vb, o_near, lse_near, *rest):
    o, lse, part, part_lse = rest[count:]
    a, b = (ka, va), (kb, vb)
    every = [(a, 0), (b, 0), (a, 1), (b, 1)]

    def store(at, block):
        o[0, at] = block

    @pl.when(meta[8] >= 1)
    def _():
        attend_rows(q, None, every, part, part_lse)
        lse[0] = blend(o_near, lse_near[0], part, part_lse[...], True, store)

    @pl.when(meta[8] < 1)
    def _():
        o[...] = o_near[...]
        lse[...] = lse_near[...]


def in_order_kernel(*refs):
    pass


def in_order(blocks, after):
    return pl.pallas_call(
        in_order_kernel,
        out_shape=[jax.ShapeDtypeStruct(block.shape, block.dtype) for block in blocks],
        in_specs=[ANY] * (len(blocks) + len(after)),
        out_specs=[ANY] * len(blocks),
        input_output_aliases={n: n for n in range(len(blocks))},
        compiler_params=params(1),
        cost_estimate=pl.CostEstimate(flops=0, bytes_accessed=0, transcendentals=0),
        name="in_order",
    )(*blocks, *after)


def halves_kernel(count, kv, *rest):
    k, v, sems = rest[count:]
    heads = k.shape[0]
    copies = [
        pltpu.make_async_copy(kv.at[pl.ds(n * heads, heads)], out, sems.at[n])
        for n, out in enumerate((k, v))
    ]
    for copy in copies:
        copy.start()
    for copy in copies:
        copy.wait()


def halves(kv, after):
    half = jax.ShapeDtypeStruct((kv.shape[0] // 2,) + kv.shape[1:], kv.dtype)
    return pl.pallas_call(
        functools.partial(halves_kernel, len(after)),
        out_shape=[half, half],
        in_specs=[ANY] * (1 + len(after)),
        out_specs=[ANY] * 2,
        scratch_shapes=[pltpu.SemaphoreType.DMA((2,))],
        compiler_params=params(1),
        cost_estimate=estimate(0),
        name="halves",
    )(kv, *after)


def lse_rows(rows):
    return -(-2 * rows // TILE // 8) * 8


def attend(body, meta, q, kv, near, after, cost):
    heads, _, rows, _ = q.shape
    block = (1, 2, rows, HEAD_DIM)
    head = pl.BlockSpec(block, lambda h: (h, 0, 0, 0))
    value = pl.BlockSpec(block, lambda h: (heads + h, 0, 0, 0))
    extra = lse_rows(rows)
    by_head = lambda h: (h, 0, 0)
    o_spec = pl.BlockSpec((1, 2 * rows, HEAD_DIM), by_head)
    lse_spec = pl.BlockSpec((1, extra, TILE), by_head)
    part_lse = pltpu.VMEM((extra, TILE), jnp.float32)
    operands, specs = [q], [head]
    for half in kv:
        apart = isinstance(half, tuple)
        operands += half if apart else [half, half]
        specs += [head, head if apart else value]
    out_shape = [
        jax.ShapeDtypeStruct((heads, 2 * rows, HEAD_DIM), jnp.float32),
        jax.ShapeDtypeStruct((heads, extra, TILE), jnp.float32),
    ]
    out_specs, scratch = [o_spec, lse_spec], []
    if body is remote_kernel:
        length = 2 * rows + 4 * extra
        out_shape = jax.ShapeDtypeStruct((heads, length, HEAD_DIM), jnp.bfloat16)
        out_specs = pl.BlockSpec((1, length, HEAD_DIM), by_head)
        scratch = [part_lse]
    if body is far_kernel:
        operands = [meta] + operands + list(near)
        specs = [SMEM] + specs + [o_spec, lse_spec]
        scratch = [pltpu.VMEM((1, 2 * rows, HEAD_DIM), jnp.float32), part_lse]
    return pl.pallas_call(
        functools.partial(body, len(after)),
        grid=(heads,),
        out_shape=out_shape,
        in_specs=specs + [ANY] * len(after),
        out_specs=out_specs,
        scratch_shapes=scratch,
        compiler_params=params(20),
        cost_estimate=estimate(cost),
        name=body.__name__[:-7],
    )(*operands, *after)


def merge_kernel(count, meta, o, lse, o_far, *rest):
    outs, scratch = rest[count : count + 4], rest[count + 4]
    rows = o.shape[1] // 2
    half = rows // 2
    extra = lse.shape[1]
    terms = o_far[0, pl.ds(2 * rows, 4 * extra)].astype(jnp.float32)
    lse_far = terms[:extra] + terms[extra : 2 * extra] + terms[2 * extra : 3 * extra]

    def store(at, block):
        scratch[at] = block

    blend(o, lse[0], o_far, lse_far, meta[8] >= 2, store)
    for j, (dx, _) in enumerate(PLACES):
        at = pl.ds(pl.multiple_of(meta[4 + j] * rows + dx * half, half), half)
        outs[j][0] = scratch[at].astype(outs[j].dtype)


def merge(meta, o, lse, o_far, after, cost):
    heads, both, _ = o.shape
    by_head = lambda h: (h, 0, 0)
    return pl.pallas_call(
        functools.partial(merge_kernel, len(after)),
        grid=(heads,),
        out_shape=[jax.ShapeDtypeStruct((heads, both // 4, HEAD_DIM), jnp.bfloat16)] * 4,
        in_specs=[SMEM]
        + [pl.BlockSpec((1,) + a.shape[1:], by_head) for a in (o, lse, o_far)]
        + [ANY] * len(after),
        out_specs=[pl.BlockSpec((1, both // 4, HEAD_DIM), by_head)] * 4,
        scratch_shapes=[pltpu.VMEM((both, HEAD_DIM), jnp.float32)],
        compiler_params=params(12),
        cost_estimate=estimate(cost),
        name="merge",
    )(meta, o, lse, o_far, *after)


def finish_kernel(firsts, group_width, meta, gate, *refs):
    pieces, out = refs[:-1], refs[-1]
    for i, piece in enumerate(pieces):
        chunk, j = divmod(i, 4)
        for h in range(piece.shape[0]):
            column = meta[j] * group_width + (firsts[chunk] + h) * HEAD_DIM
            at = pl.ds(pl.multiple_of(column, HEAD_DIM), HEAD_DIM)
            out[:, at] = (gate[:, at] * piece[h].astype(jnp.float32)).astype(out.dtype)


def finish(meta, gate, pieces, firsts, group_width, cost=0):
    rows = pieces[0].shape[1]
    whole = pl.BlockSpec(memory_space=pltpu.VMEM)
    return pl.pallas_call(
        functools.partial(finish_kernel, firsts, group_width),
        out_shape=jax.ShapeDtypeStruct((rows, 4 * group_width), jnp.bfloat16),
        in_specs=[SMEM] + [whole] * (1 + len(pieces)),
        out_specs=whole,
        compiler_params=params(16),
        cost_estimate=estimate(cost),
        name="finish",
    )(meta, gate, *pieces)


def chunk_sizes(heads):
    sizes = []
    for size in SIZES:
        if sum(sizes) + size <= heads:
            sizes.append(size)
    return sizes + [1] * (heads - sum(sizes))


def shards(queries, keys, values, level_index, plan, gate_weight):
    span = lax.axis_index("span")
    member = lax.axis_index("seq")
    x, y = member // 2, span % 2
    group_width = queries.shape[1] // 4
    group_heads = group_width // HEAD_DIM
    meta = jnp.stack(
        [2 * (x ^ dx) + (y ^ dy) for dx, dy in PLACES]
        + [y ^ dy for _, dy in PLACES]
        + [span // 2]
    ).astype(jnp.int32)
    gate = timestep_gate(level_index, plan, gate_weight, span)

    sizes = chunk_sizes(group_heads)
    firsts = [sum(sizes[:i]) for i in range(len(sizes))]
    chunks = range(len(sizes))

    sent, packed = [], []
    for first, size in zip(firsts, sizes):
        sent.append(pack(meta, queries, keys, values, first, size, group_width, packed))
        packed = [sent[-1][0]]
    last = [gate]

    q, kv, kv_up, q_down = {}, {}, {}, {}
    far, own, results = {}, {}, {}

    def exchange(blocks):
        return [blocks[0]] + [move(blocks[j], within_level(*PLACES[j])) for j in (1, 2, 3)]

    exchanged = {0: exchange(sent[0])}
    if EARLY and len(sizes) > 1:
        exchanged[1] = exchange([sent[1][0], *in_order(sent[1][1:], last)])

    def spread(i, after, cost):
        pieces = exchanged.pop(i)
        later = sent[i + 1] if i + 1 < len(sizes) and i + 1 not in exchanged else []
        q[i], kv[i], later = stack(meta, pieces, later[1:], after, cost)
        if later:
            exchanged[i + 1] = exchange([sent[i + 1][0], *later])
        kv_up[i] = move(kv[i], one_up)
        q_down[i] = move(q[i], one_down)
        kv[i] = (kv[i], move(kv[i], other_core))
        return [q[i]]

    def near(i, after, cost):
        own[i] = attend(near_kernel, meta, q[i], kv[i], None, after, cost)
        return [own[i][1]]

    def remote(i, after, cost):
        if i in APART:
            held = tuple(halves(kv_up[i], after))
            kv_up[i] = (held, tuple(move(half, other_core) for half in held))
        else:
            held = in_order([kv_up[i]], after)[0]
            kv_up[i] = (held, move(held, other_core))
        part = attend(remote_kernel, meta, q_down[i], kv_up[i], None, [], cost)
        far[i] = move(part, one_up)
        return [part]

    def own_far(i, after, cost):
        own[i] = attend(far_kernel, meta, q[i], kv_up[i], own[i], after, cost)
        return [own[i][1]]

    def close(i, after, cost):
        merged = merge(meta, *own[i], far[i], after, cost)
        results[i] = exchange(merged)
        return [merged[0]]

    steps = {"s": spread, "n": near, "r": remote, "f": own_far, "c": close}
    for step in ORDER.split():
        name, *extra = step.split("+")
        kinds = {"q": q_down, "o": far, "b": results}
        extra = [kinds[e[0]][int(e[1])] for e in extra]
        extra = [block for e in extra for block in (e[1:] if isinstance(e, list) else [e])]
        last = steps[name[0]](int(name[1]), last + extra, COSTS.get(name, 0))
    return finish(meta, gate, sum((results[i] for i in chunks), []), firsts, group_width)


def solution(mesh):
    rows = P(AXES, None)
    return jax.shard_map(
        shards,
        mesh=mesh,
        in_specs=(rows, rows, rows, P(), P(), P()),
        out_specs=rows,
        check_vma=False,
    )
```

```python
import functools
import math

import jax
import jax.numpy as jnp
from jax import lax
from jax.experimental import pallas as pl
from jax.experimental.pallas import tpu as pltpu
from jax.sharding import PartitionSpec as P

HEAD_DIM = 128
AXES = ("span", "seq")
ANY = pl.BlockSpec(memory_space=pl.ANY)
SMEM = pl.BlockSpec(memory_space=pltpu.SMEM)
MIB = 1024 * 1024
TILE = 128
SIZES = (3, 2)
APART = (0,)
COSTS = {}
EARLY = False
ORDER = "s0 n0 s1+q0 r0 f0 r1+q1 n1 f1 c0 c1"
NT = (((1,), (1,)), ((), ()))
NN = (((1,), (0,)), ((), ()))


def params(mib):
    return pltpu.CompilerParams(vmem_limit_bytes=mib * MIB)


def estimate(microseconds):
    return pl.CostEstimate(
        flops=0, bytes_accessed=int(microseconds * 3.6e6) + 1000, transcendentals=0
    )


def move(block, target):
    spans, members = lax.axis_size("span"), lax.axis_size("seq")
    route = []
    for device in range(spans * members):
        span, member = divmod(device, members)
        to_span, to_member = target(span, member)
        if 0 <= to_span < spans:
            route.append((device, to_span * members + to_member))
    return lax.ppermute(block, AXES, route)


def within_level(dx, dy):
    return lambda span, member: (span ^ dy, member ^ (2 * dx))


def other_core(span, member):
    return span, member ^ 1


def one_up(span, member):
    return span + 2, member


def one_down(span, member):
    return span - 2, member


PLACES = ((0, 0), (0, 1), (1, 0), (1, 1))


def timestep_gate(level_index, plan, gate_weight, span_number):
    noise_level = jnp.sum(
        jnp.where(jnp.arange(level_index.shape[0], dtype=jnp.int32) == span_number, level_index, 0)
    )
    timestep = jnp.sum(
        jnp.where(jnp.arange(plan.shape[0], dtype=jnp.int32) == noise_level, plan, 0)
    )
    half_freq = gate_weight.shape[0] // 2
    frequencies = jnp.exp(-math.log(10000.0) * jnp.arange(half_freq, dtype=jnp.float32) / half_freq)
    angles = timestep.astype(jnp.float32) * frequencies
    embedding = jnp.concatenate([jnp.cos(angles), jnp.sin(angles)])[None, :]
    return jnp.dot(
        embedding, gate_weight, precision=lax.Precision.HIGHEST, preferred_element_type=jnp.float32
    )


def pack_kernel(first, heads, group_width, count, q, k, v, *rest):
    outs = rest[count:]
    x, y = lax.axis_index("seq") // 2, lax.axis_index("span") % 2
    for j, (dx, dy) in enumerate(PLACES):
        group = 2 * (x ^ dx) + (y ^ dy)
        for t, ref in enumerate((q, k, v)):
            for h in range(heads):
                column = group * group_width + (first + h) * HEAD_DIM
                at = pl.ds(pl.multiple_of(column, HEAD_DIM), HEAD_DIM)
                outs[j][t * heads + h] = ref[:, at]


def pack(q, k, v, first, heads, group_width, after):
    rows = q.shape[0]
    whole = pl.BlockSpec(memory_space=pltpu.VMEM)
    return pl.pallas_call(
        functools.partial(pack_kernel, first, heads, group_width, len(after)),
        out_shape=[jax.ShapeDtypeStruct((3 * heads, rows, HEAD_DIM), q.dtype)] * 4,
        in_specs=[whole, whole, whole] + [ANY] * len(after),
        out_specs=[whole] * 4,
        compiler_params=params(60),
        cost_estimate=estimate(0),
        name="pack",
    )(q, k, v, *after)


def stack_kernel(heads, count, meta, *refs):
    pieces, outs = refs[:4], refs[4 + count :]
    (q_out, kv_out), sems = outs[:2], outs[-1]
    rows = pieces[0].shape[1]
    copies = []
    for j, (dx, _) in enumerate(PLACES):
        parity = meta[4 + j]
        at = pl.ds(dx * rows, rows)
        for t, (source, target) in enumerate(
            (
                (pieces[j].at[pl.ds(heads, 2 * heads)], kv_out.at[:, parity, at]),
                (pieces[j].at[pl.ds(0, heads)], q_out.at[:, parity, at]),
            )
        ):
            copy = pltpu.make_async_copy(source, target, sems.at[j, t])
            copy.start()
            copies.append(copy)
    for copy in copies:
        copy.wait()


def stack(meta, pieces, later, after, cost):
    triple, rows, _ = pieces[0].shape
    heads = triple // 3
    dtype = pieces[0].dtype
    outs = pl.pallas_call(
        functools.partial(stack_kernel, heads, len(later) + len(after)),
        out_shape=[
            jax.ShapeDtypeStruct((heads, 2, 2 * rows, HEAD_DIM), dtype),
            jax.ShapeDtypeStruct((2 * heads, 2, 2 * rows, HEAD_DIM), dtype),
        ]
        + [jax.ShapeDtypeStruct(block.shape, block.dtype) for block in later],
        in_specs=[SMEM] + [ANY] * (4 + len(later) + len(after)),
        out_specs=[ANY] * (2 + len(later)),
        scratch_shapes=[pltpu.SemaphoreType.DMA((4, 2))],
        input_output_aliases={5 + n: 2 + n for n in range(len(later))},
        compiler_params=params(8),
        cost_estimate=estimate(cost),
        name="stack",
    )(meta, *pieces, *later, *after)
    return outs[0], outs[1], outs[2:]


def softmax_part(q, keys, values):
    scale = math.log2(math.e) / math.sqrt(HEAD_DIM)
    scores = [lax.dot_general(q, k, NT, preferred_element_type=jnp.float32) for k in keys]
    peak = functools.reduce(jnp.maximum, scores).max(axis=1, keepdims=True)
    peak = peak * scale
    weights = [jnp.exp2(s * scale - peak) for s in scores]
    total = functools.reduce(jnp.add, weights).sum(axis=1, keepdims=True)
    out = functools.reduce(
        jnp.add,
        [
            lax.dot_general(w.astype(jnp.bfloat16), v, NN, preferred_element_type=jnp.float32)
            for w, v in zip(weights, values)
        ],
    )
    return out / total, peak + jnp.log2(total)


def attend_rows(q_ref, p, blocks, o_ref, lse_ref):
    rows, q = q_ref.shape[2], q_ref[0, p or 0]
    if p is None:
        rows, p, q = 2 * rows, 0, q_ref[0].reshape(2 * rows, HEAD_DIM)
    out, lse = softmax_part(
        q, [kv[0][0, i] for kv, i in blocks], [kv[1][0, i] for kv, i in blocks]
    )
    o_ref[0, pl.ds(p * rows, rows)] = out.astype(o_ref.dtype)
    for t in range(rows // TILE):
        column = jnp.broadcast_to(lse[t * TILE : (t + 1) * TILE], (TILE, TILE))
        lse_ref[pl.ds(p * (rows // TILE) + t, 1)] = column.T[:1]


def remote_kernel(count, q, ka, va, kb, vb, *rest):
    o, lse = rest[count:]
    a, b = (ka, va), (kb, vb)
    every = [(a, 0), (b, 0), (a, 1), (b, 1)]
    attend_rows(q, 0, every, o, lse)
    attend_rows(q, 1, every[2:], o, lse)
    left, terms = lse[...], []
    for _ in range(3):
        terms.append(left.astype(jnp.bfloat16))
        left = left - terms[-1].astype(jnp.float32)
    terms.append(jnp.zeros_like(terms[0]))
    last = 2 * q.shape[2]
    o[0, pl.ds(last, 4 * lse.shape[0])] = jnp.concatenate(
        [term.astype(jnp.float32) for term in terms], axis=0
    ).astype(jnp.bfloat16)


def near_kernel(count, q, ka, va, kb, vb, *rest):
    o, lse = rest[count:]
    a, b = (ka, va), (kb, vb)
    own = [(a, 0), (b, 0), (a, 1), (b, 1)]
    attend_rows(q, 0, own[:2], o, lse.at[0])
    attend_rows(q, 1, own, o, lse.at[0])


def blend(first, first_lse, other, other_lse, usable, store):
    share = jnp.where(usable, 1.0, 0.0) / (1.0 + jnp.exp2(first_lse - other_lse))
    for row in range(first.shape[1] // TILE):
        at = pl.ds(row * TILE, TILE)
        weight = jnp.broadcast_to(share[row : row + 1], (HEAD_DIM, TILE)).T
        start = first[0, at]
        store(at, start + weight * (other[0, at].astype(jnp.float32) - start))
    more = jnp.log2(1.0 + jnp.exp2(-jnp.abs(first_lse - other_lse)))
    return jnp.where(usable, jnp.maximum(first_lse, other_lse) + more, first_lse)


def far_kernel(count, meta, q, ka, va, kb, vb, o_near, lse_near, *rest):
    o, lse, part, part_lse = rest[count:]
    a, b = (ka, va), (kb, vb)
    every = [(a, 0), (b, 0), (a, 1), (b, 1)]

    def store(at, block):
        o[0, at] = block

    @pl.when(meta[8] >= 1)
    def _():
        attend_rows(q, None, every, part, part_lse)
        lse[0] = blend(o_near, lse_near[0], part, part_lse[...], True, store)

    @pl.when(meta[8] < 1)
    def _():
        o[...] = o_near[...]
        lse[...] = lse_near[...]


def in_order_kernel(*refs):
    pass


def in_order(blocks, after):
    return pl.pallas_call(
        in_order_kernel,
        out_shape=[jax.ShapeDtypeStruct(block.shape, block.dtype) for block in blocks],
        in_specs=[ANY] * (len(blocks) + len(after)),
        out_specs=[ANY] * len(blocks),
        input_output_aliases={n: n for n in range(len(blocks))},
        compiler_params=params(1),
        cost_estimate=pl.CostEstimate(flops=0, bytes_accessed=0, transcendentals=0),
        name="in_order",
    )(*blocks, *after)


def halves_kernel(count, kv, *rest):
    k, v, sems = rest[count:]
    heads = k.shape[0]
    copies = [
        pltpu.make_async_copy(kv.at[pl.ds(n * heads, heads)], out, sems.at[n])
        for n, out in enumerate((k, v))
    ]
    for copy in copies:
        copy.start()
    for copy in copies:
        copy.wait()


def halves(kv, after):
    half = jax.ShapeDtypeStruct((kv.shape[0] // 2,) + kv.shape[1:], kv.dtype)
    return pl.pallas_call(
        functools.partial(halves_kernel, len(after)),
        out_shape=[half, half],
        in_specs=[ANY] * (1 + len(after)),
        out_specs=[ANY] * 2,
        scratch_shapes=[pltpu.SemaphoreType.DMA((2,))],
        compiler_params=params(1),
        cost_estimate=estimate(0),
        name="halves",
    )(kv, *after)


def lse_rows(rows):
    return -(-2 * rows // TILE // 8) * 8


def attend(body, meta, q, kv, near, after, cost):
    heads, _, rows, _ = q.shape
    block = (1, 2, rows, HEAD_DIM)
    head = pl.BlockSpec(block, lambda h: (h, 0, 0, 0))
    value = pl.BlockSpec(block, lambda h: (heads + h, 0, 0, 0))
    extra = lse_rows(rows)
    by_head = lambda h: (h, 0, 0)
    o_spec = pl.BlockSpec((1, 2 * rows, HEAD_DIM), by_head)
    lse_spec = pl.BlockSpec((1, extra, TILE), by_head)
    part_lse = pltpu.VMEM((extra, TILE), jnp.float32)
    operands, specs = [q], [head]
    for half in kv:
        apart = isinstance(half, tuple)
        operands += half if apart else [half, half]
        specs += [head, head if apart else value]
    out_shape = [
        jax.ShapeDtypeStruct((heads, 2 * rows, HEAD_DIM), jnp.float32),
        jax.ShapeDtypeStruct((heads, extra, TILE), jnp.float32),
    ]
    out_specs, scratch = [o_spec, lse_spec], []
    if body is remote_kernel:
        length = 2 * rows + 4 * extra
        out_shape = jax.ShapeDtypeStruct((heads, length, HEAD_DIM), jnp.bfloat16)
        out_specs = pl.BlockSpec((1, length, HEAD_DIM), by_head)
        scratch = [part_lse]
    if body is far_kernel:
        operands = [meta] + operands + list(near)
        specs = [SMEM] + specs + [o_spec, lse_spec]
        scratch = [pltpu.VMEM((1, 2 * rows, HEAD_DIM), jnp.float32), part_lse]
    return pl.pallas_call(
        functools.partial(body, len(after)),
        grid=(heads,),
        out_shape=out_shape,
        in_specs=specs + [ANY] * len(after),
        out_specs=out_specs,
        scratch_shapes=scratch,
        compiler_params=params(20),
        cost_estimate=estimate(cost),
        name=body.__name__[:-7],
    )(*operands, *after)


def merge_kernel(count, meta, o, lse, o_far, *rest):
    outs, scratch = rest[count : count + 4], rest[count + 4]
    rows = o.shape[1] // 2
    half = rows // 2
    extra = lse.shape[1]
    terms = o_far[0, pl.ds(2 * rows, 4 * extra)].astype(jnp.float32)
    lse_far = terms[:extra] + terms[extra : 2 * extra] + terms[2 * extra : 3 * extra]

    def store(at, block):
        scratch[at] = block

    blend(o, lse[0], o_far, lse_far, meta[8] >= 2, store)
    for j, (dx, _) in enumerate(PLACES):
        at = pl.ds(pl.multiple_of(meta[4 + j] * rows + dx * half, half), half)
        outs[j][0] = scratch[at].astype(outs[j].dtype)


def merge(meta, o, lse, o_far, after, cost):
    heads, both, _ = o.shape
    by_head = lambda h: (h, 0, 0)
    return pl.pallas_call(
        functools.partial(merge_kernel, len(after)),
        grid=(heads,),
        out_shape=[jax.ShapeDtypeStruct((heads, both // 4, HEAD_DIM), jnp.bfloat16)] * 4,
        in_specs=[SMEM]
        + [pl.BlockSpec((1,) + a.shape[1:], by_head) for a in (o, lse, o_far)]
        + [ANY] * len(after),
        out_specs=[pl.BlockSpec((1, both // 4, HEAD_DIM), by_head)] * 4,
        scratch_shapes=[pltpu.VMEM((both, HEAD_DIM), jnp.float32)],
        compiler_params=params(12),
        cost_estimate=estimate(cost),
        name="merge",
    )(meta, o, lse, o_far, *after)


def finish_kernel(first, group_width, count, meta, gate, *refs):
    pieces, (out, rows, sems) = refs[:4], refs[4 + count :]
    copies = []
    for j, piece in enumerate(pieces):
        for h in range(piece.shape[0]):
            column = meta[j] * group_width + (first + h) * HEAD_DIM
            at = pl.ds(pl.multiple_of(column, HEAD_DIM), HEAD_DIM)
            rows[j, h] = (gate[:, at] * piece[h].astype(jnp.float32)).astype(rows.dtype)
            copy = pltpu.make_async_copy(rows.at[j, h], out.at[:, at], sems.at[j, h])
            copy.start()
            copies.append(copy)
    for copy in copies:
        copy.wait()


def finish(meta, gate, pieces, first, group_width, base):
    heads, rows, _ = pieces[0].shape
    whole = pl.BlockSpec(memory_space=pltpu.VMEM)
    base = [] if base is None else [base]
    return pl.pallas_call(
        functools.partial(finish_kernel, first, group_width, len(base)),
        out_shape=jax.ShapeDtypeStruct((rows, 4 * group_width), jnp.bfloat16),
        in_specs=[SMEM] + [whole] * 5 + [ANY] * len(base),
        out_specs=ANY,
        scratch_shapes=[
            pltpu.VMEM((4, heads, rows, HEAD_DIM), jnp.bfloat16),
            pltpu.SemaphoreType.DMA((4, heads)),
        ],
        input_output_aliases={6: 0} if base else {},
        compiler_params=params(16),
        cost_estimate=estimate(0),
        name="finish",
    )(meta, gate, *pieces, *base)


def chunk_sizes(heads):
    sizes = []
    for size in SIZES:
        if sum(sizes) + size <= heads:
            sizes.append(size)
    return sizes + [1] * (heads - sum(sizes))


def shards(queries, keys, values, level_index, plan, gate_weight):
    span = lax.axis_index("span")
    member = lax.axis_index("seq")
    x, y = member // 2, span % 2
    group_width = queries.shape[1] // 4
    group_heads = group_width // HEAD_DIM
    meta = jnp.stack(
        [2 * (x ^ dx) + (y ^ dy) for dx, dy in PLACES]
        + [y ^ dy for _, dy in PLACES]
        + [span // 2]
    ).astype(jnp.int32)
    gate = timestep_gate(level_index, plan, gate_weight, span)

    sizes = chunk_sizes(group_heads)
    firsts = [sum(sizes[:i]) for i in range(len(sizes))]
    chunks = range(len(sizes))

    sent, packed = [], []
    for first, size in zip(firsts, sizes):
        sent.append(pack(queries, keys, values, first, size, group_width, packed))
        packed = [sent[-1][0]]
    last = [gate]

    q, kv, kv_up, q_down = {}, {}, {}, {}
    far, own, results = {}, {}, {}

    def exchange(blocks):
        return [blocks[0]] + [move(blocks[j], within_level(*PLACES[j])) for j in (1, 2, 3)]

    exchanged = {0: exchange(sent[0])}
    if EARLY and len(sizes) > 1:
        exchanged[1] = exchange([sent[1][0], *in_order(sent[1][1:], last)])

    def spread(i, after, cost):
        pieces = exchanged.pop(i)
        later = sent[i + 1] if i + 1 < len(sizes) and i + 1 not in exchanged else []
        q[i], kv[i], later = stack(meta, pieces, later[1:], after, cost)
        if later:
            exchanged[i + 1] = exchange([sent[i + 1][0], *later])
        kv_up[i] = move(kv[i], one_up)
        q_down[i] = move(q[i], one_down)
        kv[i] = (kv[i], move(kv[i], other_core))
        return [q[i]]

    def near(i, after, cost):
        own[i] = attend(near_kernel, meta, q[i], kv[i], None, after, cost)
        return [own[i][1]]

    def remote(i, after, cost):
        if i in APART:
            held = tuple(halves(kv_up[i], after))
            kv_up[i] = (held, tuple(move(half, other_core) for half in held))
        else:
            held = in_order([kv_up[i]], after)[0]
            kv_up[i] = (held, move(held, other_core))
        part = attend(remote_kernel, meta, q_down[i], kv_up[i], None, [], cost)
        far[i] = move(part, one_up)
        return [part]

    def own_far(i, after, cost):
        own[i] = attend(far_kernel, meta, q[i], kv_up[i], own[i], after, cost)
        return [own[i][1]]

    def close(i, after, cost):
        merged = merge(meta, *own[i], far[i], after, cost)
        results[i] = exchange(merged)
        return [merged[0]]

    steps = {"s": spread, "n": near, "r": remote, "f": own_far, "c": close}
    for step in ORDER.split():
        name, *extra = step.split("+")
        kinds = {"q": q_down, "o": far, "b": results}
        extra = [kinds[e[0]][int(e[1])] for e in extra]
        extra = [block for e in extra for block in (e[1:] if isinstance(e, list) else [e])]
        last = steps[name[0]](int(name[1]), last + extra, COSTS.get(name, 0))
    out = None
    for i, first in enumerate(firsts):
        out = finish(meta, gate, results[i], first, group_width, out)
    return out


def solution(mesh):
    rows = P(AXES, None)
    return jax.shard_map(
        shards,
        mesh=mesh,
        in_specs=(rows, rows, rows, P(), P(), P()),
        out_specs=rows,
        check_vma=False,
    )
```

```python
import functools
import math

import jax
import jax.numpy as jnp
from jax import lax
from jax.experimental import pallas as pl
from jax.experimental.pallas import tpu as pltpu
from jax.sharding import PartitionSpec as P

HEAD_DIM = 128
AXES = ("span", "seq")
ANY = pl.BlockSpec(memory_space=pl.ANY)
SMEM = pl.BlockSpec(memory_space=pltpu.SMEM)
MIB = 1024 * 1024
TILE = 128
SIZES = (3, 2)
APART = (0,)
COSTS = {}
EARLY = False
ORDER = "s0 n0 s1+q0 r0 f0 r1+q1 n1 f1 c0 c1"
NT = (((1,), (1,)), ((), ()))
NN = (((1,), (0,)), ((), ()))


def params(mib):
    return pltpu.CompilerParams(vmem_limit_bytes=mib * MIB)


def estimate(microseconds):
    return pl.CostEstimate(
        flops=0, bytes_accessed=int(microseconds * 3.6e6) + 1000, transcendentals=0
    )


def move(block, target):
    spans, members = lax.axis_size("span"), lax.axis_size("seq")
    route = []
    for device in range(spans * members):
        span, member = divmod(device, members)
        to_span, to_member = target(span, member)
        if 0 <= to_span < spans:
            route.append((device, to_span * members + to_member))
    return lax.ppermute(block, AXES, route)


def within_level(dx, dy):
    return lambda span, member: (span ^ dy, member ^ (2 * dx))


def other_core(span, member):
    return span, member ^ 1


def one_up(span, member):
    return span + 2, member


def one_down(span, member):
    return span - 2, member


PLACES = ((0, 0), (1, 1), (0, 1), (1, 0))


def timestep_gate(level_index, plan, gate_weight, span_number):
    noise_level = jnp.sum(
        jnp.where(jnp.arange(level_index.shape[0], dtype=jnp.int32) == span_number, level_index, 0)
    )
    timestep = jnp.sum(
        jnp.where(jnp.arange(plan.shape[0], dtype=jnp.int32) == noise_level, plan, 0)
    )
    half_freq = gate_weight.shape[0] // 2
    frequencies = jnp.exp(-math.log(10000.0) * jnp.arange(half_freq, dtype=jnp.float32) / half_freq)
    angles = timestep.astype(jnp.float32) * frequencies
    embedding = jnp.concatenate([jnp.cos(angles), jnp.sin(angles)])[None, :]
    return jnp.dot(
        embedding, gate_weight, precision=lax.Precision.HIGHEST, preferred_element_type=jnp.float32
    )


def pack_kernel(first, heads, group_width, count, q, k, v, *rest):
    outs = rest[count:]
    x, y = lax.axis_index("seq") // 2, lax.axis_index("span") % 2
    for j, (dx, dy) in enumerate(PLACES):
        group = 2 * (x ^ dx) + (y ^ dy)
        for t, ref in enumerate((q, k, v)):
            for h in range(heads):
                column = group * group_width + (first + h) * HEAD_DIM
                at = pl.ds(pl.multiple_of(column, HEAD_DIM), HEAD_DIM)
                outs[j][t * heads + h] = ref[:, at]


def pack(q, k, v, first, heads, group_width, after):
    rows = q.shape[0]
    whole = pl.BlockSpec(memory_space=pltpu.VMEM)
    return pl.pallas_call(
        functools.partial(pack_kernel, first, heads, group_width, len(after)),
        out_shape=[jax.ShapeDtypeStruct((3 * heads, rows, HEAD_DIM), q.dtype)] * 4,
        in_specs=[whole, whole, whole] + [ANY] * len(after),
        out_specs=[whole] * 4,
        compiler_params=params(60),
        cost_estimate=estimate(0),
        name="pack",
    )(q, k, v, *after)


def stack_kernel(heads, count, meta, *refs):
    pieces, outs = refs[:4], refs[4 + count :]
    (q_out, kv_out), sems = outs[:2], outs[-1]
    rows = pieces[0].shape[1]
    copies = []
    for j, (dx, _) in enumerate(PLACES):
        parity = meta[4 + j]
        at = pl.ds(dx * rows, rows)
        for t, (source, target) in enumerate(
            (
                (pieces[j].at[pl.ds(heads, 2 * heads)], kv_out.at[:, parity, at]),
                (pieces[j].at[pl.ds(0, heads)], q_out.at[:, parity, at]),
            )
        ):
            copy = pltpu.make_async_copy(source, target, sems.at[j, t])
            copy.start()
            copies.append(copy)
    for copy in copies:
        copy.wait()


def stack(meta, pieces, later, after, cost):
    triple, rows, _ = pieces[0].shape
    heads = triple // 3
    dtype = pieces[0].dtype
    outs = pl.pallas_call(
        functools.partial(stack_kernel, heads, len(later) + len(after)),
        out_shape=[
            jax.ShapeDtypeStruct((heads, 2, 2 * rows, HEAD_DIM), dtype),
            jax.ShapeDtypeStruct((2 * heads, 2, 2 * rows, HEAD_DIM), dtype),
        ]
        + [jax.ShapeDtypeStruct(block.shape, block.dtype) for block in later],
        in_specs=[SMEM] + [ANY] * (4 + len(later) + len(after)),
        out_specs=[ANY] * (2 + len(later)),
        scratch_shapes=[pltpu.SemaphoreType.DMA((4, 2))],
        input_output_aliases={5 + n: 2 + n for n in range(len(later))},
        compiler_params=params(8),
        cost_estimate=estimate(cost),
        name="stack",
    )(meta, *pieces, *later, *after)
    return outs[0], outs[1], outs[2:]


def softmax_part(q, keys, values):
    scale = math.log2(math.e) / math.sqrt(HEAD_DIM)
    scores = [lax.dot_general(q, k, NT, preferred_element_type=jnp.float32) for k in keys]
    peak = functools.reduce(jnp.maximum, scores).max(axis=1, keepdims=True)
    peak = peak * scale
    weights = [jnp.exp2(s * scale - peak) for s in scores]
    total = functools.reduce(jnp.add, weights).sum(axis=1, keepdims=True)
    out = functools.reduce(
        jnp.add,
        [
            lax.dot_general(w.astype(jnp.bfloat16), v, NN, preferred_element_type=jnp.float32)
            for w, v in zip(weights, values)
        ],
    )
    return out / total, peak + jnp.log2(total)


def attend_rows(q_ref, p, blocks, o_ref, lse_ref):
    rows, q = q_ref.shape[2], q_ref[0, p or 0]
    if p is None:
        rows, p, q = 2 * rows, 0, q_ref[0].reshape(2 * rows, HEAD_DIM)
    out, lse = softmax_part(
        q, [kv[0][0, i] for kv, i in blocks], [kv[1][0, i] for kv, i in blocks]
    )
    o_ref[0, pl.ds(p * rows, rows)] = out.astype(o_ref.dtype)
    for t in range(rows // TILE):
        column = jnp.broadcast_to(lse[t * TILE : (t + 1) * TILE], (TILE, TILE))
        lse_ref[pl.ds(p * (rows // TILE) + t, 1)] = column.T[:1]


def remote_kernel(count, q, ka, va, kb, vb, *rest):
    o, lse = rest[count:]
    a, b = (ka, va), (kb, vb)
    every = [(a, 0), (b, 0), (a, 1), (b, 1)]
    attend_rows(q, 0, every, o, lse)
    attend_rows(q, 1, every[2:], o, lse)
    left, terms = lse[...], []
    for _ in range(3):
        terms.append(left.astype(jnp.bfloat16))
        left = left - terms[-1].astype(jnp.float32)
    terms.append(jnp.zeros_like(terms[0]))
    last = 2 * q.shape[2]
    o[0, pl.ds(last, 4 * lse.shape[0])] = jnp.concatenate(
        [term.astype(jnp.float32) for term in terms], axis=0
    ).astype(jnp.bfloat16)


def near_kernel(count, q, ka, va, kb, vb, *rest):
    o, lse = rest[count:]
    a, b = (ka, va), (kb, vb)
    own = [(a, 0), (b, 0), (a, 1), (b, 1)]
    attend_rows(q, 0, own[:2], o, lse.at[0])
    attend_rows(q, 1, own, o, lse.at[0])


def blend(first, first_lse, other, other_lse, usable, store):
    share = jnp.where(usable, 1.0, 0.0) / (1.0 + jnp.exp2(first_lse - other_lse))
    for row in range(first.shape[1] // TILE):
        at = pl.ds(row * TILE, TILE)
        weight = jnp.broadcast_to(share[row : row + 1], (HEAD_DIM, TILE)).T
        start = first[0, at]
        store(at, start + weight * (other[0, at].astype(jnp.float32) - start))
    more = jnp.log2(1.0 + jnp.exp2(-jnp.abs(first_lse - other_lse)))
    return jnp.where(usable, jnp.maximum(first_lse, other_lse) + more, first_lse)


def far_kernel(count, meta, q, ka, va, kb, vb, o_near, lse_near, *rest):
    o, lse, part, part_lse = rest[count:]
    a, b = (ka, va), (kb, vb)
    every = [(a, 0), (b, 0), (a, 1), (b, 1)]

    def store(at, block):
        o[0, at] = block

    @pl.when(meta[8] >= 1)
    def _():
        attend_rows(q, None, every, part, part_lse)
        lse[0] = blend(o_near, lse_near[0], part, part_lse[...], True, store)

    @pl.when(meta[8] < 1)
    def _():
        o[...] = o_near[...]
        lse[...] = lse_near[...]


def in_order_kernel(*refs):
    pass


def in_order(blocks, after):
    return pl.pallas_call(
        in_order_kernel,
        out_shape=[jax.ShapeDtypeStruct(block.shape, block.dtype) for block in blocks],
        in_specs=[ANY] * (len(blocks) + len(after)),
        out_specs=[ANY] * len(blocks),
        input_output_aliases={n: n for n in range(len(blocks))},
        compiler_params=params(1),
        cost_estimate=pl.CostEstimate(flops=0, bytes_accessed=0, transcendentals=0),
        name="in_order",
    )(*blocks, *after)


def halves_kernel(count, kv, *rest):
    k, v, sems = rest[count:]
    heads = k.shape[0]
    copies = [
        pltpu.make_async_copy(kv.at[pl.ds(n * heads, heads)], out, sems.at[n])
        for n, out in enumerate((k, v))
    ]
    for copy in copies:
        copy.start()
    for copy in copies:
        copy.wait()


def halves(kv, after):
    half = jax.ShapeDtypeStruct((kv.shape[0] // 2,) + kv.shape[1:], kv.dtype)
    return pl.pallas_call(
        functools.partial(halves_kernel, len(after)),
        out_shape=[half, half],
        in_specs=[ANY] * (1 + len(after)),
        out_specs=[ANY] * 2,
        scratch_shapes=[pltpu.SemaphoreType.DMA((2,))],
        compiler_params=params(1),
        cost_estimate=estimate(0),
        name="halves",
    )(kv, *after)


def lse_rows(rows):
    return -(-2 * rows // TILE // 8) * 8


def attend(body, meta, q, kv, near, after, cost):
    heads, _, rows, _ = q.shape
    block = (1, 2, rows, HEAD_DIM)
    head = pl.BlockSpec(block, lambda h: (h, 0, 0, 0))
    value = pl.BlockSpec(block, lambda h: (heads + h, 0, 0, 0))
    extra = lse_rows(rows)
    by_head = lambda h: (h, 0, 0)
    o_spec = pl.BlockSpec((1, 2 * rows, HEAD_DIM), by_head)
    lse_spec = pl.BlockSpec((1, extra, TILE), by_head)
    part_lse = pltpu.VMEM((extra, TILE), jnp.float32)
    operands, specs = [q], [head]
    for half in kv:
        apart = isinstance(half, tuple)
        operands += half if apart else [half, half]
        specs += [head, head if apart else value]
    out_shape = [
        jax.ShapeDtypeStruct((heads, 2 * rows, HEAD_DIM), jnp.float32),
        jax.ShapeDtypeStruct((heads, extra, TILE), jnp.float32),
    ]
    out_specs, scratch = [o_spec, lse_spec], []
    if body is remote_kernel:
        length = 2 * rows + 4 * extra
        out_shape = jax.ShapeDtypeStruct((heads, length, HEAD_DIM), jnp.bfloat16)
        out_specs = pl.BlockSpec((1, length, HEAD_DIM), by_head)
        scratch = [part_lse]
    if body is far_kernel:
        operands = [meta] + operands + list(near)
        specs = [SMEM] + specs + [o_spec, lse_spec]
        scratch = [pltpu.VMEM((1, 2 * rows, HEAD_DIM), jnp.float32), part_lse]
    return pl.pallas_call(
        functools.partial(body, len(after)),
        grid=(heads,),
        out_shape=out_shape,
        in_specs=specs + [ANY] * len(after),
        out_specs=out_specs,
        scratch_shapes=scratch,
        compiler_params=params(20),
        cost_estimate=estimate(cost),
        name=body.__name__[:-7],
    )(*operands, *after)


def merge_kernel(count, meta, o, lse, o_far, *rest):
    outs, scratch = rest[count : count + 4], rest[count + 4]
    rows = o.shape[1] // 2
    half = rows // 2
    extra = lse.shape[1]
    terms = o_far[0, pl.ds(2 * rows, 4 * extra)].astype(jnp.float32)
    lse_far = terms[:extra] + terms[extra : 2 * extra] + terms[2 * extra : 3 * extra]

    def store(at, block):
        scratch[at] = block

    blend(o, lse[0], o_far, lse_far, meta[8] >= 2, store)
    for j, (dx, _) in enumerate(PLACES):
        at = pl.ds(pl.multiple_of(meta[4 + j] * rows + dx * half, half), half)
        outs[j][0] = scratch[at].astype(outs[j].dtype)


def merge(meta, o, lse, o_far, after, cost):
    heads, both, _ = o.shape
    by_head = lambda h: (h, 0, 0)
    return pl.pallas_call(
        functools.partial(merge_kernel, len(after)),
        grid=(heads,),
        out_shape=[jax.ShapeDtypeStruct((heads, both // 4, HEAD_DIM), jnp.bfloat16)] * 4,
        in_specs=[SMEM]
        + [pl.BlockSpec((1,) + a.shape[1:], by_head) for a in (o, lse, o_far)]
        + [ANY] * len(after),
        out_specs=[pl.BlockSpec((1, both // 4, HEAD_DIM), by_head)] * 4,
        scratch_shapes=[pltpu.VMEM((both, HEAD_DIM), jnp.float32)],
        compiler_params=params(12),
        cost_estimate=estimate(cost),
        name="merge",
    )(meta, o, lse, o_far, *after)


def finish_kernel(first, group_width, count, meta, gate, *refs):
    pieces, (out, rows, sems) = refs[:4], refs[4 + count :]
    copies = []
    for j, piece in enumerate(pieces):
        for h in range(piece.shape[0]):
            column = meta[j] * group_width + (first + h) * HEAD_DIM
            at = pl.ds(pl.multiple_of(column, HEAD_DIM), HEAD_DIM)
            rows[j, h] = (gate[:, at] * piece[h].astype(jnp.float32)).astype(rows.dtype)
            copy = pltpu.make_async_copy(rows.at[j, h], out.at[:, at], sems.at[j, h])
            copy.start()
            copies.append(copy)
    for copy in copies:
        copy.wait()


def finish(meta, gate, pieces, first, group_width, base):
    heads, rows, _ = pieces[0].shape
    whole = pl.BlockSpec(memory_space=pltpu.VMEM)
    base = [] if base is None else [base]
    return pl.pallas_call(
        functools.partial(finish_kernel, first, group_width, len(base)),
        out_shape=jax.ShapeDtypeStruct((rows, 4 * group_width), jnp.bfloat16),
        in_specs=[SMEM] + [whole] * 5 + [ANY] * len(base),
        out_specs=ANY,
        scratch_shapes=[
            pltpu.VMEM((4, heads, rows, HEAD_DIM), jnp.bfloat16),
            pltpu.SemaphoreType.DMA((4, heads)),
        ],
        input_output_aliases={6: 0} if base else {},
        compiler_params=params(16),
        cost_estimate=estimate(0),
        name="finish",
    )(meta, gate, *pieces, *base)


def chunk_sizes(heads):
    sizes = []
    for size in SIZES:
        if sum(sizes) + size <= heads:
            sizes.append(size)
    return sizes + [1] * (heads - sum(sizes))


def shards(queries, keys, values, level_index, plan, gate_weight):
    span = lax.axis_index("span")
    member = lax.axis_index("seq")
    x, y = member // 2, span % 2
    group_width = queries.shape[1] // 4
    group_heads = group_width // HEAD_DIM
    meta = jnp.stack(
        [2 * (x ^ dx) + (y ^ dy) for dx, dy in PLACES]
        + [y ^ dy for _, dy in PLACES]
        + [span // 2]
    ).astype(jnp.int32)
    gate = timestep_gate(level_index, plan, gate_weight, span)

    sizes = chunk_sizes(group_heads)
    firsts = [sum(sizes[:i]) for i in range(len(sizes))]
    chunks = range(len(sizes))

    sent, packed = [], []
    for first, size in zip(firsts, sizes):
        sent.append(pack(queries, keys, values, first, size, group_width, packed))
        packed = [sent[-1][0]]
    last = [gate]

    q, kv, kv_up, q_down = {}, {}, {}, {}
    far, own, results = {}, {}, {}

    def exchange(blocks):
        return [blocks[0]] + [move(blocks[j], within_level(*PLACES[j])) for j in (1, 2, 3)]

    exchanged = {0: exchange(sent[0])}
    if EARLY and len(sizes) > 1:
        exchanged[1] = exchange([sent[1][0], *in_order(sent[1][1:], last)])

    def spread(i, after, cost):
        pieces = exchanged.pop(i)
        later = sent[i + 1] if i + 1 < len(sizes) and i + 1 not in exchanged else []
        q[i], kv[i], later = stack(meta, pieces, later[1:], after, cost)
        if later:
            exchanged[i + 1] = exchange([sent[i + 1][0], *later])
        kv_up[i] = move(kv[i], one_up)
        q_down[i] = move(q[i], one_down)
        kv[i] = (kv[i], move(kv[i], other_core))
        return [q[i]]

    def near(i, after, cost):
        own[i] = attend(near_kernel, meta, q[i], kv[i], None, after, cost)
        return [own[i][1]]

    def remote(i, after, cost):
        if i in APART:
            held = tuple(halves(kv_up[i], after))
            kv_up[i] = (held, tuple(move(half, other_core) for half in held))
        else:
            held = in_order([kv_up[i]], after)[0]
            kv_up[i] = (held, move(held, other_core))
        part = attend(remote_kernel, meta, q_down[i], kv_up[i], None, [], cost)
        far[i] = move(part, one_up)
        return [part]

    def own_far(i, after, cost):
        own[i] = attend(far_kernel, meta, q[i], kv_up[i], own[i], after, cost)
        return [own[i][1]]

    def close(i, after, cost):
        merged = merge(meta, *own[i], far[i], after, cost)
        results[i] = exchange(merged)
        return [merged[0]]

    steps = {"s": spread, "n": near, "r": remote, "f": own_far, "c": close}
    for step in ORDER.split():
        name, *extra = step.split("+")
        kinds = {"q": q_down, "o": far, "b": results}
        extra = [kinds[e[0]][int(e[1])] for e in extra]
        extra = [block for e in extra for block in (e[1:] if isinstance(e, list) else [e])]
        last = steps[name[0]](int(name[1]), last + extra, COSTS.get(name, 0))
    out = None
    for i, first in enumerate(firsts):
        out = finish(meta, gate, results[i], first, group_width, out)
    return out


def solution(mesh):
    rows = P(AXES, None)
    return jax.shard_map(
        shards,
        mesh=mesh,
        in_specs=(rows, rows, rows, P(), P(), P()),
        out_specs=rows,
        check_vma=False,
    )
```

```python
import functools
import math

import jax
import jax.numpy as jnp
from jax import lax
from jax.experimental import pallas as pl
from jax.experimental.pallas import tpu as pltpu
from jax.sharding import PartitionSpec as P

HEAD_DIM = 128
AXES = ("span", "seq")
ANY = pl.BlockSpec(memory_space=pl.ANY)
SMEM = pl.BlockSpec(memory_space=pltpu.SMEM)
MIB = 1024 * 1024
TILE = 128
SIZES = (3, 2)
APART = (0,)
COSTS = {}
EARLY = False
ORDER = "s0 n0 s1+q0 r0 f0 r1+q1 n1 f1 c0 c1"
NT = (((1,), (1,)), ((), ()))
NN = (((1,), (0,)), ((), ()))


def params(mib):
    return pltpu.CompilerParams(vmem_limit_bytes=mib * MIB)


def estimate(microseconds):
    return pl.CostEstimate(
        flops=0, bytes_accessed=int(microseconds * 3.6e6) + 1000, transcendentals=0
    )


def move(block, target):
    spans, members = lax.axis_size("span"), lax.axis_size("seq")
    route = []
    for device in range(spans * members):
        span, member = divmod(device, members)
        to_span, to_member = target(span, member)
        if 0 <= to_span < spans:
            route.append((device, to_span * members + to_member))
    return lax.ppermute(block, AXES, route)


def within_level(dx, dy):
    return lambda span, member: (span ^ dy, member ^ (2 * dx))


def other_core(span, member):
    return span, member ^ 1


def one_up(span, member):
    return span + 2, member


def one_down(span, member):
    return span - 2, member


PLACES = ((0, 0), (1, 1), (0, 1), (1, 0))


def timestep_gate(level_index, plan, gate_weight, span_number):
    noise_level = jnp.sum(
        jnp.where(jnp.arange(level_index.shape[0], dtype=jnp.int32) == span_number, level_index, 0)
    )
    timestep = jnp.sum(
        jnp.where(jnp.arange(plan.shape[0], dtype=jnp.int32) == noise_level, plan, 0)
    )
    half_freq = gate_weight.shape[0] // 2
    frequencies = jnp.exp(-math.log(10000.0) * jnp.arange(half_freq, dtype=jnp.float32) / half_freq)
    angles = timestep.astype(jnp.float32) * frequencies
    embedding = jnp.concatenate([jnp.cos(angles), jnp.sin(angles)])[None, :]
    return jnp.dot(
        embedding, gate_weight, precision=lax.Precision.HIGHEST, preferred_element_type=jnp.float32
    )


def pack_kernel(first, heads, group_width, count, q, k, v, *rest):
    outs = rest[count:]
    x, y = lax.axis_index("seq") // 2, lax.axis_index("span") % 2
    for j, (dx, dy) in enumerate(PLACES):
        group = 2 * (x ^ dx) + (y ^ dy)
        for t, ref in enumerate((q, k, v)):
            for h in range(heads):
                column = group * group_width + (first + h) * HEAD_DIM
                at = pl.ds(pl.multiple_of(column, HEAD_DIM), HEAD_DIM)
                outs[j][t * heads + h] = ref[:, at]


def pack(q, k, v, first, heads, group_width, after):
    rows = q.shape[0]
    whole = pl.BlockSpec(memory_space=pltpu.VMEM)
    return pl.pallas_call(
        functools.partial(pack_kernel, first, heads, group_width, len(after)),
        out_shape=[jax.ShapeDtypeStruct((3 * heads, rows, HEAD_DIM), q.dtype)] * 4,
        in_specs=[whole, whole, whole] + [ANY] * len(after),
        out_specs=[whole] * 4,
        compiler_params=params(60),
        cost_estimate=estimate(0),
        name="pack",
    )(q, k, v, *after)


def stack_kernel(heads, count, meta, *refs):
    pieces, outs = refs[:4], refs[4 + count :]
    (q_out, kv_out), sems = outs[:2], outs[-1]
    rows = pieces[0].shape[1]
    copies = []
    for j, (dx, _) in enumerate(PLACES):
        parity = meta[4 + j]
        at = pl.ds(dx * rows, rows)
        for t, (source, target) in enumerate(
            (
                (pieces[j].at[pl.ds(heads, 2 * heads)], kv_out.at[:, parity, at]),
                (pieces[j].at[pl.ds(0, heads)], q_out.at[:, parity, at]),
            )
        ):
            copy = pltpu.make_async_copy(source, target, sems.at[j, t])
            copy.start()
            copies.append(copy)
    for copy in copies:
        copy.wait()


def stack(meta, pieces, later, after, cost):
    triple, rows, _ = pieces[0].shape
    heads = triple // 3
    dtype = pieces[0].dtype
    outs = pl.pallas_call(
        functools.partial(stack_kernel, heads, len(later) + len(after)),
        out_shape=[
            jax.ShapeDtypeStruct((heads, 2, 2 * rows, HEAD_DIM), dtype),
            jax.ShapeDtypeStruct((2 * heads, 2, 2 * rows, HEAD_DIM), dtype),
        ]
        + [jax.ShapeDtypeStruct(block.shape, block.dtype) for block in later],
        in_specs=[SMEM] + [ANY] * (4 + len(later) + len(after)),
        out_specs=[ANY] * (2 + len(later)),
        scratch_shapes=[pltpu.SemaphoreType.DMA((4, 2))],
        input_output_aliases={5 + n: 2 + n for n in range(len(later))},
        compiler_params=params(8),
        cost_estimate=estimate(cost),
        name="stack",
    )(meta, *pieces, *later, *after)
    return outs[0], outs[1], outs[2:]


def softmax_part(q, keys, values):
    scale = math.log2(math.e) / math.sqrt(HEAD_DIM)
    scores = [lax.dot_general(q, k, NT, preferred_element_type=jnp.float32) for k in keys]
    peak = functools.reduce(jnp.maximum, scores).max(axis=1, keepdims=True)
    peak = peak * scale
    weights = [jnp.exp2(s * scale - peak) for s in scores]
    total = functools.reduce(jnp.add, weights).sum(axis=1, keepdims=True)
    out = functools.reduce(
        jnp.add,
        [
            lax.dot_general(w.astype(jnp.bfloat16), v, NN, preferred_element_type=jnp.float32)
            for w, v in zip(weights, values)
        ],
    )
    return out / total, peak + jnp.log2(total)


def attend_rows(q_ref, p, blocks, o_ref, lse_ref):
    rows, q = q_ref.shape[2], q_ref[0, p or 0]
    if p is None:
        rows, p, q = 2 * rows, 0, q_ref[0].reshape(2 * rows, HEAD_DIM)
    out, lse = softmax_part(
        q, [kv[0][0, i] for kv, i in blocks], [kv[1][0, i] for kv, i in blocks]
    )
    o_ref[0, pl.ds(p * rows, rows)] = out.astype(o_ref.dtype)
    for t in range(rows // TILE):
        column = jnp.broadcast_to(lse[t * TILE : (t + 1) * TILE], (TILE, TILE))
        lse_ref[pl.ds(p * (rows // TILE) + t, 1)] = column.T[:1]


def attend_with_extra(q_ref, joint, extra, half, o_ref, lse_ref):
    rows = q_ref.shape[2]
    scale = math.log2(math.e) / math.sqrt(HEAD_DIM)

    def scores_of(q, blocks):
        keys = [kv[0][0, i] for kv, i in blocks]
        return [lax.dot_general(q, k, NT, preferred_element_type=jnp.float32) for k in keys]

    def sums(scores, peak, blocks):
        weights = [jnp.exp2(s * scale - peak) for s in scores]
        values = [kv[1][0, i] for kv, i in blocks]
        out = [
            lax.dot_general(w.astype(jnp.bfloat16), v, NN, preferred_element_type=jnp.float32)
            for w, v in zip(weights, values)
        ]
        total = functools.reduce(jnp.add, weights).sum(axis=1, keepdims=True)
        return total, functools.reduce(jnp.add, out)

    def top(scores):
        return functools.reduce(jnp.maximum, scores).max(axis=1, keepdims=True) * scale

    every = scores_of(q_ref[0].reshape(2 * rows, HEAD_DIM), joint)
    more = scores_of(q_ref[0, half], extra)
    peak = top(every)
    peaks = [peak[:rows], peak[rows:]]
    peaks[half] = jnp.maximum(peaks[half], top(more))
    total, out = sums(every, jnp.concatenate(peaks, axis=0), joint)
    more_total, more_out = sums(more, peaks[half], extra)
    for p in range(2):
        part = slice(p * rows, (p + 1) * rows)
        sum_p, out_p = total[part], out[part]
        if p == half:
            sum_p, out_p = sum_p + more_total, out_p + more_out
        o_ref[0, pl.ds(p * rows, rows)] = (out_p / sum_p).astype(o_ref.dtype)
        lse = peaks[p] + jnp.log2(sum_p)
        for t in range(rows // TILE):
            column = jnp.broadcast_to(lse[t * TILE : (t + 1) * TILE], (TILE, TILE))
            lse_ref[pl.ds(p * (rows // TILE) + t, 1)] = column.T[:1]


def remote_kernel(count, q, ka, va, kb, vb, *rest):
    o, lse = rest[count:]
    a, b = (ka, va), (kb, vb)
    every = [(a, 0), (b, 0), (a, 1), (b, 1)]
    attend_with_extra(q, every[2:], every[:2], 0, o, lse)
    left, terms = lse[...], []
    for _ in range(3):
        terms.append(left.astype(jnp.bfloat16))
        left = left - terms[-1].astype(jnp.float32)
    terms.append(jnp.zeros_like(terms[0]))
    last = 2 * q.shape[2]
    o[0, pl.ds(last, 4 * lse.shape[0])] = jnp.concatenate(
        [term.astype(jnp.float32) for term in terms], axis=0
    ).astype(jnp.bfloat16)


def near_kernel(count, q, ka, va, kb, vb, *rest):
    o, lse = rest[count:]
    a, b = (ka, va), (kb, vb)
    own = [(a, 0), (b, 0), (a, 1), (b, 1)]
    attend_rows(q, 0, own[:2], o, lse.at[0])
    attend_rows(q, 1, own, o, lse.at[0])


def blend(first, first_lse, other, other_lse, usable, store):
    share = jnp.where(usable, 1.0, 0.0) / (1.0 + jnp.exp2(first_lse - other_lse))
    for row in range(first.shape[1] // TILE):
        at = pl.ds(row * TILE, TILE)
        weight = jnp.broadcast_to(share[row : row + 1], (HEAD_DIM, TILE)).T
        start = first[0, at]
        store(at, start + weight * (other[0, at].astype(jnp.float32) - start))
    more = jnp.log2(1.0 + jnp.exp2(-jnp.abs(first_lse - other_lse)))
    return jnp.where(usable, jnp.maximum(first_lse, other_lse) + more, first_lse)


def far_kernel(count, meta, q, ka, va, kb, vb, o_near, lse_near, *rest):
    o, lse, part, part_lse = rest[count:]
    a, b = (ka, va), (kb, vb)
    every = [(a, 0), (b, 0), (a, 1), (b, 1)]

    def store(at, block):
        o[0, at] = block

    @pl.when(meta[8] >= 1)
    def _():
        attend_rows(q, None, every, part, part_lse)
        lse[0] = blend(o_near, lse_near[0], part, part_lse[...], True, store)

    @pl.when(meta[8] < 1)
    def _():
        o[...] = o_near[...]
        lse[...] = lse_near[...]


def in_order_kernel(*refs):
    pass


def in_order(blocks, after):
    return pl.pallas_call(
        in_order_kernel,
        out_shape=[jax.ShapeDtypeStruct(block.shape, block.dtype) for block in blocks],
        in_specs=[ANY] * (len(blocks) + len(after)),
        out_specs=[ANY] * len(blocks),
        input_output_aliases={n: n for n in range(len(blocks))},
        compiler_params=params(1),
        cost_estimate=pl.CostEstimate(flops=0, bytes_accessed=0, transcendentals=0),
        name="in_order",
    )(*blocks, *after)


def halves_kernel(count, kv, *rest):
    k, v, sems = rest[count:]
    heads = k.shape[0]
    copies = [
        pltpu.make_async_copy(kv.at[pl.ds(n * heads, heads)], out, sems.at[n])
        for n, out in enumerate((k, v))
    ]
    for copy in copies:
        copy.start()
    for copy in copies:
        copy.wait()


def halves(kv, after):
    half = jax.ShapeDtypeStruct((kv.shape[0] // 2,) + kv.shape[1:], kv.dtype)
    return pl.pallas_call(
        functools.partial(halves_kernel, len(after)),
        out_shape=[half, half],
        in_specs=[ANY] * (1 + len(after)),
        out_specs=[ANY] * 2,
        scratch_shapes=[pltpu.SemaphoreType.DMA((2,))],
        compiler_params=params(1),
        cost_estimate=estimate(0),
        name="halves",
    )(kv, *after)


def lse_rows(rows):
    return -(-2 * rows // TILE // 8) * 8


def attend(body, meta, q, kv, near, after, cost):
    heads, _, rows, _ = q.shape
    block = (1, 2, rows, HEAD_DIM)
    head = pl.BlockSpec(block, lambda h: (h, 0, 0, 0))
    value = pl.BlockSpec(block, lambda h: (heads + h, 0, 0, 0))
    extra = lse_rows(rows)
    by_head = lambda h: (h, 0, 0)
    o_spec = pl.BlockSpec((1, 2 * rows, HEAD_DIM), by_head)
    lse_spec = pl.BlockSpec((1, extra, TILE), by_head)
    part_lse = pltpu.VMEM((extra, TILE), jnp.float32)
    operands, specs = [q], [head]
    for half in kv:
        apart = isinstance(half, tuple)
        operands += half if apart else [half, half]
        specs += [head, head if apart else value]
    out_shape = [
        jax.ShapeDtypeStruct((heads, 2 * rows, HEAD_DIM), jnp.float32),
        jax.ShapeDtypeStruct((heads, extra, TILE), jnp.float32),
    ]
    out_specs, scratch = [o_spec, lse_spec], []
    if body is remote_kernel:
        length = 2 * rows + 4 * extra
        out_shape = jax.ShapeDtypeStruct((heads, length, HEAD_DIM), jnp.bfloat16)
        out_specs = pl.BlockSpec((1, length, HEAD_DIM), by_head)
        scratch = [part_lse]
    if body is far_kernel:
        operands = [meta] + operands + list(near)
        specs = [SMEM] + specs + [o_spec, lse_spec]
        scratch = [pltpu.VMEM((1, 2 * rows, HEAD_DIM), jnp.float32), part_lse]
    return pl.pallas_call(
        functools.partial(body, len(after)),
        grid=(heads,),
        out_shape=out_shape,
        in_specs=specs + [ANY] * len(after),
        out_specs=out_specs,
        scratch_shapes=scratch,
        compiler_params=params(20),
        cost_estimate=estimate(cost),
        name=body.__name__[:-7],
    )(*operands, *after)


def merge_kernel(count, meta, o, lse, o_far, *rest):
    outs, scratch = rest[count : count + 4], rest[count + 4]
    rows = o.shape[1] // 2
    half = rows // 2
    extra = lse.shape[1]
    terms = o_far[0, pl.ds(2 * rows, 4 * extra)].astype(jnp.float32)
    lse_far = terms[:extra] + terms[extra : 2 * extra] + terms[2 * extra : 3 * extra]

    def store(at, block):
        scratch[at] = block

    blend(o, lse[0], o_far, lse_far, meta[8] >= 2, store)
    for j, (dx, _) in enumerate(PLACES):
        at = pl.ds(pl.multiple_of(meta[4 + j] * rows + dx * half, half), half)
        outs[j][0] = scratch[at].astype(outs[j].dtype)


def merge(meta, o, lse, o_far, after, cost):
    heads, both, _ = o.shape
    by_head = lambda h: (h, 0, 0)
    return pl.pallas_call(
        functools.partial(merge_kernel, len(after)),
        grid=(heads,),
        out_shape=[jax.ShapeDtypeStruct((heads, both // 4, HEAD_DIM), jnp.bfloat16)] * 4,
        in_specs=[SMEM]
        + [pl.BlockSpec((1,) + a.shape[1:], by_head) for a in (o, lse, o_far)]
        + [ANY] * len(after),
        out_specs=[pl.BlockSpec((1, both // 4, HEAD_DIM), by_head)] * 4,
        scratch_shapes=[pltpu.VMEM((both, HEAD_DIM), jnp.float32)],
        compiler_params=params(12),
        cost_estimate=estimate(cost),
        name="merge",
    )(meta, o, lse, o_far, *after)


def finish_kernel(first, group_width, count, meta, gate, *refs):
    pieces, (out, rows, sems) = refs[:4], refs[4 + count :]
    copies = []
    for j, piece in enumerate(pieces):
        for h in range(piece.shape[0]):
            column = meta[j] * group_width + (first + h) * HEAD_DIM
            at = pl.ds(pl.multiple_of(column, HEAD_DIM), HEAD_DIM)
            rows[j, h] = (gate[:, at] * piece[h].astype(jnp.float32)).astype(rows.dtype)
            copy = pltpu.make_async_copy(rows.at[j, h], out.at[:, at], sems.at[j, h])
            copy.start()
            copies.append(copy)
    for copy in copies:
        copy.wait()


def finish(meta, gate, pieces, first, group_width, base):
    heads, rows, _ = pieces[0].shape
    whole = pl.BlockSpec(memory_space=pltpu.VMEM)
    base = [] if base is None else [base]
    return pl.pallas_call(
        functools.partial(finish_kernel, first, group_width, len(base)),
        out_shape=jax.ShapeDtypeStruct((rows, 4 * group_width), jnp.bfloat16),
        in_specs=[SMEM] + [whole] * 5 + [ANY] * len(base),
        out_specs=ANY,
        scratch_shapes=[
            pltpu.VMEM((4, heads, rows, HEAD_DIM), jnp.bfloat16),
            pltpu.SemaphoreType.DMA((4, heads)),
        ],
        input_output_aliases={6: 0} if base else {},
        compiler_params=params(16),
        cost_estimate=estimate(0),
        name="finish",
    )(meta, gate, *pieces, *base)


def chunk_sizes(heads):
    sizes = []
    for size in SIZES:
        if sum(sizes) + size <= heads:
            sizes.append(size)
    return sizes + [1] * (heads - sum(sizes))


def shards(queries, keys, values, level_index, plan, gate_weight):
    span = lax.axis_index("span")
    member = lax.axis_index("seq")
    x, y = member // 2, span % 2
    group_width = queries.shape[1] // 4
    group_heads = group_width // HEAD_DIM
    meta = jnp.stack(
        [2 * (x ^ dx) + (y ^ dy) for dx, dy in PLACES]
        + [y ^ dy for _, dy in PLACES]
        + [span // 2]
    ).astype(jnp.int32)
    gate = timestep_gate(level_index, plan, gate_weight, span)

    sizes = chunk_sizes(group_heads)
    firsts = [sum(sizes[:i]) for i in range(len(sizes))]
    chunks = range(len(sizes))

    sent, packed = [], []
    for first, size in zip(firsts, sizes):
        sent.append(pack(queries, keys, values, first, size, group_width, packed))
        packed = [sent[-1][0]]
    last = [gate]

    q, kv, kv_up, q_down = {}, {}, {}, {}
    far, own, results = {}, {}, {}

    def exchange(blocks):
        return [blocks[0]] + [move(blocks[j], within_level(*PLACES[j])) for j in (1, 2, 3)]

    exchanged = {0: exchange(sent[0])}
    if EARLY and len(sizes) > 1:
        exchanged[1] = exchange([sent[1][0], *in_order(sent[1][1:], last)])

    def spread(i, after, cost):
        pieces = exchanged.pop(i)
        later = sent[i + 1] if i + 1 < len(sizes) and i + 1 not in exchanged else []
        q[i], kv[i], later = stack(meta, pieces, later[1:], after, cost)
        if later:
            exchanged[i + 1] = exchange([sent[i + 1][0], *later])
        kv_up[i] = move(kv[i], one_up)
        q_down[i] = move(q[i], one_down)
        kv[i] = (kv[i], move(kv[i], other_core))
        return [q[i]]

    def near(i, after, cost):
        own[i] = attend(near_kernel, meta, q[i], kv[i], None, after, cost)
        return [own[i][1]]

    def remote(i, after, cost):
        if i in APART:
            held = tuple(halves(kv_up[i], after))
            kv_up[i] = (held, tuple(move(half, other_core) for half in held))
        else:
            held = in_order([kv_up[i]], after)[0]
            kv_up[i] = (held, move(held, other_core))
        part = attend(remote_kernel, meta, q_down[i], kv_up[i], None, [], cost)
        far[i] = move(part, one_up)
        return [part]

    def own_far(i, after, cost):
        own[i] = attend(far_kernel, meta, q[i], kv_up[i], own[i], after, cost)
        return [own[i][1]]

    def close(i, after, cost):
        merged = merge(meta, *own[i], far[i], after, cost)
        results[i] = exchange(merged)
        return [merged[0]]

    steps = {"s": spread, "n": near, "r": remote, "f": own_far, "c": close}
    for step in ORDER.split():
        name, *extra = step.split("+")
        kinds = {"q": q_down, "o": far, "b": results}
        extra = [kinds[e[0]][int(e[1])] for e in extra]
        extra = [block for e in extra for block in (e[1:] if isinstance(e, list) else [e])]
        last = steps[name[0]](int(name[1]), last + extra, COSTS.get(name, 0))
    out = None
    for i, first in enumerate(firsts):
        out = finish(meta, gate, results[i], first, group_width, out)
    return out


def solution(mesh):
    rows = P(AXES, None)
    return jax.shard_map(
        shards,
        mesh=mesh,
        in_specs=(rows, rows, rows, P(), P(), P()),
        out_specs=rows,
        check_vma=False,
    )
```
